32 devices in a mesh: seq: 2 (over x), fsdp: 16 (over z, y, core).
Axes of the slice: x: 2, y: 2, z: 4, core: 2. Of those that a mesh axis runs over, the one named last changes fastest.
Arguments:
- inputs: bfloat16 [32, 1024, 768], P('fsdp', 'seq'), may hold values from -6 to 6
- out_grad: bfloat16 [32, 1024, 768], P('fsdp', 'seq'), may hold values from -6 to 6
- first_gain: bfloat16 [768], P(('seq', 'fsdp')), may hold values from 0.099609375 to 1.8984375
- first_shift: bfloat16 [768], P(('seq', 'fsdp')), may hold values from -3 to 3
- w_qkv: bfloat16 [768, 2304], P(('seq', 'fsdp')), may hold values from -0.21875 to 0.21875
- b_query: bfloat16 [768], P(('seq', 'fsdp')), may hold values from -3 to 3
- b_value: bfloat16 [768], P(('seq', 'fsdp')), may hold values from -3 to 3
- w_proj: bfloat16 [768, 768], P(('seq', 'fsdp')), may hold values from -0.875 to 0.875
- b_proj: bfloat16 [768], P(('seq', 'fsdp')), may hold values from -3 to 3
- second_gain: bfloat16 [768], P(('seq', 'fsdp')), may hold values from 0.099609375 to 1.8984375
- second_shift: bfloat16 [768], P(('seq', 'fsdp')), may hold values from -3 to 3
- w_up: bfloat16 [768, 3072], P(('seq', 'fsdp')), may hold values from -0.21875 to 0.21875
- b_up: bfloat16 [3072], P(('seq', 'fsdp')), may hold values from -3 to 3
- w_down: bfloat16 [3072, 768], P(('seq', 'fsdp')), may hold values from -0.21875 to 0.21875
- b_down: bfloat16 [768], P(('seq', 'fsdp')), may hold values from -3 to 3
Outputs:
- outputs: bfloat16 [32, 1024, 768], P('fsdp', 'seq')
- input_grad: float32 [32, 1024, 768], P('fsdp', 'seq')
- grad_first_gain: float32 [768], P(('seq', 'fsdp'))
- grad_first_shift: float32 [768], P(('seq', 'fsdp'))
- grad_w_qkv: float32 [768, 2304], P(('seq', 'fsdp'))
- grad_b_query: float32 [768], P(('seq', 'fsdp'))
- grad_b_value: float32 [768], P(('seq', 'fsdp'))
- grad_w_proj: float32 [768, 768], P(('seq', 'fsdp'))
- grad_b_proj: float32 [768], P(('seq', 'fsdp'))
- grad_second_gain: float32 [768], P(('seq', 'fsdp'))
- grad_second_shift: float32 [768], P(('seq', 'fsdp'))
- grad_w_up: float32 [768, 3072], P(('seq', 'fsdp'))
- grad_b_up: float32 [3072], P(('seq', 'fsdp'))
- grad_w_down: float32 [3072, 768], P(('seq', 'fsdp'))
- grad_b_down: float32 [768], P(('seq', 'fsdp'))
The draws below stay inside these ranges and needn't reach their ends.
All inputs are finite; a program needn't handle non-finite values.
Results may differ from the reference program's by a relative error of at most 0.013.
Values may be sent and summed in bfloat16 or wider, within the bound.
No kernel may reach another device: no remote copies, remote signals or barrier semaphores. Data moves between devices by JAX's collectives and lax.ppermute only.
A program may use at most 192 MiB of HBM per device.

```python
import jax
import jax.numpy as jnp
from jax import lax

D = 768
H = 12
HD = 64
FF = 3072
SEQ_LEN = 1024
SEQS = 32
QB = 512


def shard_levels(rng, dims, split, smallest, largest):
    level, own = 1.0, jax.random.fold_in(rng, 6)
    for dim, shards_of in split:
        steps = jnp.exp(jax.random.uniform(jax.random.fold_in(own, dim), (shards_of,), jnp.float32, smallest / len(split), largest / len(split)))
        level = level * jnp.repeat(steps, dims[dim] // shards_of).reshape([-1 if axis == dim else 1 for axis in range(len(dims))])
    return level


def gaussian(stream_key, extent, scale, bound, shards=(), kind=jnp.bfloat16):
    entries = scale * jax.random.normal(stream_key, extent, jnp.float32)
    if shards:
        entries = entries * shard_levels(stream_key, extent, shards, -0.22, 0.18)
    return jnp.clip(entries, -bound, bound).astype(kind)


def setup_inputs(seed: int = 0) -> dict:
    seeds = jax.random.split(jax.random.key(seed), 16)
    inputs = gaussian(seeds[0], (SEQS, SEQ_LEN, D), 1.0, 6.0, ((0, 16), (1, 2)))
    out_grad = gaussian(seeds[1], (SEQS, SEQ_LEN, D), 1.0, 6.0, ((0, 16), (1, 2)))
    first_gain = jnp.clip(1.0 + 0.18 * jax.random.normal(seeds[2], (D,), jnp.float32), 0.099609375, 1.8984375).astype(jnp.bfloat16)
    first_shift = gaussian(seeds[3], (D,), 0.3, 3.0, ((0, 32),))
    w_qkv = gaussian(seeds[4], (D, 3 * D), D ** -0.5, 0.21875, ((0, 32),))
    b_query = gaussian(seeds[5], (D,), 0.3, 3.0, ((0, 32),))
    b_value = gaussian(seeds[6], (D,), 0.3, 3.0, ((0, 32),))
    w_proj = gaussian(seeds[7], (D, D), (D // 16) ** -0.5, 0.875, ((0, 32),))
    b_proj = gaussian(seeds[8], (D,), 0.3, 3.0, ((0, 32),))
    second_gain = jnp.clip(1.0 + 0.18 * jax.random.normal(seeds[9], (D,), jnp.float32), 0.099609375, 1.8984375).astype(jnp.bfloat16)
    second_shift = gaussian(seeds[10], (D,), 0.3, 3.0, ((0, 32),))
    w_up = gaussian(seeds[11], (D, FF), D ** -0.5, 0.21875, ((0, 32),))
    b_up = gaussian(seeds[12], (FF,), 0.3, 3.0, ((0, 32),))
    w_down = gaussian(seeds[13], (FF, D), (FF // 4) ** -0.5, 0.21875, ((0, 32),))
    b_down = gaussian(seeds[14], (D,), 0.3, 3.0, ((0, 32),))
    return dict(inputs=inputs, out_grad=out_grad, first_gain=first_gain, first_shift=first_shift, w_qkv=w_qkv, b_query=b_query, b_value=b_value, w_proj=w_proj, b_proj=b_proj, second_gain=second_gain, second_shift=second_shift, w_up=w_up, b_up=b_up, w_down=w_down, b_down=b_down)


@jax.custom_vjp
def low(v):
    return lax.optimization_barrier(v.astype(jnp.bfloat16)).astype(jnp.float32)

@jax.custom_vjp
def low_back(v):
    return v

def low_keep(v):
    return (low(v), None)

def low_pass(kept, grad):
    return (grad,)

def back_keep(v):
    return (v, None)

def back_low(kept, grad):
    return (low(grad),)
low.defvjp(low_keep, low_pass)
low_back.defvjp(back_keep, back_low)
EPSILON = 1e-05
HIGHEST = lax.Precision.HIGHEST

def layer_norm(values, gain, shift):
    centre = values - lax.optimization_barrier(jnp.mean(values, axis=-1, keepdims=True))
    spread = lax.optimization_barrier(jnp.mean(centre * centre, axis=-1, keepdims=True))
    return centre * lax.rsqrt(spread + EPSILON) * gain + shift

def attend_block(query_rows, key_matrix_rows, value_matrix_rows, start):
    scores = jnp.einsum('qhd,khd->hqk', query_rows, key_matrix_rows, precision=HIGHEST) * HD ** (-0.5)
    scores = low_back(scores)
    row_place = start + jnp.arange(query_rows.shape[0], dtype=jnp.int32)
    col_place = jnp.arange(key_matrix_rows.shape[0], dtype=jnp.int32)
    causal = col_place[None, :] <= row_place[:, None]
    scores = jnp.where(causal[None], scores, -1e+30)
    weights = low(jax.nn.softmax(scores, axis=-1))
    return jnp.einsum('hqk,khd->qhd', weights, value_matrix_rows, precision=HIGHEST)

def forward(tokens, params):
    first_gain, first_shift, w_qkv, b_query, b_value, w_proj, b_proj, second_gain, second_shift, w_up, b_up, w_down, b_down = params
    normed = low(layer_norm(tokens, first_gain, first_shift))
    packed = jnp.dot(normed, w_qkv, precision=HIGHEST)
    packed = packed + jnp.concatenate([b_query, jnp.zeros_like(b_query), b_value])
    packed = low(low_back(packed))
    heads = packed.reshape(SEQ_LEN, 3, H, HD)
    key_all = heads[:, 1]
    value_all = heads[:, 2]
    block_count = SEQ_LEN // QB
    query_blocks = heads[:, 0].reshape(block_count, QB, H, HD)
    starts = jnp.arange(block_count, dtype=jnp.int32) * QB

    def one_block(item):
        return attend_block(item[0], key_all, value_all, item[1])
    attended = lax.map(jax.checkpoint(one_block), (query_blocks, starts))
    attended = low(low_back(attended.reshape(SEQ_LEN, D)))
    branch = low_back(jnp.dot(attended, w_proj, precision=HIGHEST) + b_proj)
    middle = tokens + branch
    normed_two = low(layer_norm(middle, second_gain, second_shift))
    hidden_pre = low_back(jnp.dot(normed_two, w_up, precision=HIGHEST) + b_up)
    hidden = low(jax.nn.gelu(hidden_pre, approximate=True))
    branch_two = low_back(jnp.dot(hidden, w_down, precision=HIGHEST) + b_down)
    return middle + branch_two

def reference(inputs, out_grad, first_gain, first_shift, w_qkv, b_query, b_value, w_proj, b_proj, second_gain, second_shift, w_up, b_up, w_down, b_down):
    params = tuple((item.astype(jnp.float32) for item in (first_gain, first_shift, w_qkv, b_query, b_value, w_proj, b_proj, second_gain, second_shift, w_up, b_up, w_down, b_down)))

    def one_sequence(totals, item):
        seq_in, seq_cot = item
        result, pullback = jax.vjp(forward, seq_in.astype(jnp.float32), params)
        grad_in, grad_params = pullback(seq_cot.astype(jnp.float32))
        totals = jax.tree.map(jnp.add, totals, grad_params)
        return (totals, (result.astype(jnp.bfloat16), grad_in))
    zeros = tuple((jnp.zeros_like(item) for item in params))
    totals, (outputs, input_grad) = lax.scan(one_sequence, zeros, (inputs, out_grad))
    return (outputs, input_grad, totals[0], totals[1], totals[2], totals[3], totals[4], totals[5], totals[6], totals[7], totals[8], totals[9], totals[10], totals[11], totals[12])
```

```python
import functools

import jax
import jax.numpy as jnp
from jax import lax
from jax.experimental import pallas as pl
from jax.experimental.pallas import tpu as pltpu
from jax.sharding import PartitionSpec as P

H = 12
HD = 64
PAIR = 2 * HD
EPSILON = 1e-05
F32 = jnp.float32
BF16 = jnp.bfloat16
NT = (((1,), (1,)), ((), ()))
NN = (((1,), (0,)), ((), ()))
SUB = 256
VMEM = 56 * 1024 * 1024


def dot(a, b, dims=NN):
    return lax.dot_general(a, b, dims, preferred_element_type=F32)


def head_lanes(x, head):
    lane = lax.broadcasted_iota(jnp.int32, x.shape, 1)
    return jnp.where((lane // HD) == head, x, jnp.zeros_like(x))


def masked(scores, start):
    key = lax.broadcasted_iota(jnp.int32, scores.shape, 0)
    query = lax.broadcasted_iota(jnp.int32, scores.shape, 1) + start
    return jnp.where(key <= query, scores, -1e30)


def forward_tile(q, k, v, causal):
    q = q * jnp.asarray(HD**-0.5, q.dtype)
    v_t = v.T
    rows, keys = q.shape[0], k.shape[0]
    outs, stats = [], []
    for head in range(2):
        q_h = head_lanes(q, head)
        v_h = v_t[head * HD : (head + 1) * HD]
        out_h, stat_h = [], []
        for start in range(0, rows, SUB):
            used = start + SUB if causal else keys
            s = dot(k[:used], q_h[start : start + SUB], NT)
            if causal:
                s = masked(s, start)
            top = jnp.max(s, axis=0, keepdims=True)
            e = jnp.exp(s - top)
            total = jnp.sum(e, axis=0, keepdims=True)
            out_h.append(dot(v_h[:, :used], e.astype(BF16)) / total)
            stat_h.append(top + jnp.log(total))
        outs.append(jnp.concatenate(out_h, axis=1))
        stats.append(jnp.concatenate(stat_h, axis=1))
    return jnp.concatenate(outs, axis=0).T, jnp.concatenate(stats, axis=0)


def backward_tile(q, k, v, g, stat, delta, causal):
    q = q * jnp.asarray(HD**-0.5, q.dtype)
    k_t = k.T
    rows, keys = q.shape[0], k.shape[0]
    dq_heads = []
    pieces = [None] * (keys // SUB), [None] * (keys // SUB)

    def add(which, start, value):
        for i in range(value.shape[0] // SUB):
            part = value[i * SUB : (i + 1) * SUB]
            old = pieces[which][start + i]
            pieces[which][start + i] = part if old is None else old + part

    for head in range(2):
        q_h = head_lanes(q, head)
        g_h = head_lanes(g, head)
        k_h = k_t[head * HD : (head + 1) * HD]
        dq_h = []
        for start in range(0, rows, SUB):
            used = start + SUB if causal else keys
            cols = slice(start, start + SUB)
            s = dot(k[:used], q_h[cols], NT)
            if causal:
                s = masked(s, start)
            p = jnp.exp(s - stat[head : head + 1, cols])
            dp = dot(v[:used], g_h[cols], NT)
            ds = (p * (dp - delta[head : head + 1, cols])).astype(BF16)
            add(1, 0, dot(p.astype(BF16), g_h[cols]))
            add(0, 0, dot(ds, q_h[cols]))
            dq_h.append(dot(k_h[:, :used], ds))
        dq_heads.append(jnp.concatenate(dq_h, axis=1))
    dq = jnp.concatenate(dq_heads, axis=0).T * HD**-0.5
    return dq, jnp.concatenate(pieces[0], axis=0), jnp.concatenate(pieces[1], axis=0)


def local_forward_kernel(q, k, v, o, stat):
    out, lse = forward_tile(q[0], k[0], v[0], True)
    o[0] = out.astype(BF16)
    stat[0, 0] = lse


def cross_forward_kernel(late, q, k, v, r1, r2, o, stat):
    is_late = late[0] == 1
    r = r1[0]
    out, lse = forward_tile(
        jnp.where(is_late, q[0], r),
        jnp.where(is_late, r, k[0]),
        jnp.where(is_late, r2[0], v[0]),
        False,
    )
    o[0] = out.astype(BF16)
    stat[0, 0] = lse


def spread(rows, size):
    a = jnp.broadcast_to(rows[0:1], (HD, size))
    b = jnp.broadcast_to(rows[1:2], (HD, size))
    return jnp.concatenate([a, b], axis=0).T


def merge_kernel(late, o1, l1, o2, l2, o3, l3, o, stat):
    near = pl.program_id(0) < pl.num_programs(0) // 2
    is_late = late[0] == 1
    first = l1[0, 0]
    second = jnp.where(near, l2[0, 0], l3[0, 0])
    gap = second - first
    weight = jnp.where(is_late, 1.0 / (1.0 + jnp.exp(-gap)), 0.0)
    both = jnp.maximum(first, second) + jnp.log(1.0 + jnp.exp(-jnp.abs(gap)))
    stat[0, 0] = jnp.where(is_late, both, first)
    a = o1[0].astype(F32)
    b = jnp.where(near, o2[0], o3[0]).astype(F32)
    o[0] = (a + spread(weight, a.shape[0]) * (b - a)).astype(BF16)


def delta_kernel(o, g, delta):
    prod = (o[0].astype(F32) * g[0].astype(F32)).T
    delta[0, 0] = jnp.concatenate(
        [
            jnp.sum(prod[:HD], axis=0, keepdims=True),
            jnp.sum(prod[HD:], axis=0, keepdims=True),
        ],
        axis=0,
    )


def local_backward_kernel(q, k, v, g, stat, delta, dq, dk, dv):
    a, b, c = backward_tile(q[0], k[0], v[0], g[0], stat[0, 0], delta[0, 0], True)
    dq[0] = a.astype(BF16)
    dk[0] = b.astype(BF16)
    dv[0] = c.astype(BF16)


def cross_backward_kernel(
    late, q, k, v, r1, r2, g, rg, stat, delta, rstat, rdelta, send, keep
):
    is_late = late[0] == 1
    r = r1[0]
    a, b, c = backward_tile(
        jnp.where(is_late, q[0], r),
        jnp.where(is_late, r, k[0]),
        jnp.where(is_late, r2[0], v[0]),
        jnp.where(is_late, g[0], rg[0]),
        jnp.where(is_late, stat[0, 0], rstat[0, 0]),
        jnp.where(is_late, delta[0, 0], rdelta[0, 0]),
        False,
    )
    a, b = a.astype(BF16), b.astype(BF16)
    place = pl.program_id(0) * PAIR
    span = pl.num_programs(0) * PAIR
    send[0, :, pl.ds(pl.multiple_of(place, PAIR), PAIR)] = jnp.where(is_late, b, a)
    send[0, :, pl.ds(pl.multiple_of(span + place, PAIR), PAIR)] = c.astype(BF16)
    keep[0] = jnp.where(is_late, a, b)


def cols(length, b0=0, shift=0, low=lambda p: p):
    return pl.BlockSpec((1, length, PAIR), lambda p: (b0, 0, low(p) + shift))


def stats(length, shift=0, low=lambda p: p):
    return pl.BlockSpec((1, 1, 2, length), lambda p: (0, low(p) + shift, 0, 0))


SCALAR = pl.BlockSpec(memory_space=pltpu.SMEM)


def call(kernel, grid, ins, outs, shapes, cost, name, scratch=()):
    return pl.pallas_call(
        kernel,
        grid=grid,
        in_specs=ins,
        out_specs=outs,
        out_shape=shapes,
        scratch_shapes=scratch,
        compiler_params=pltpu.CompilerParams(vmem_limit_bytes=VMEM),
        cost_estimate=pl.CostEstimate(
            flops=cost, bytes_accessed=cost // 256, transcendentals=cost // 256
        ),
        name=name,
    )


def gelu_parts(u):
    c = (2.0 / jnp.pi) ** 0.5
    u2 = u * u
    t = jnp.tanh(u * (c + (c * 0.044715) * u2))
    half = 0.5 + 0.5 * t
    value = u * half
    slope = half + 0.5 * u * (1.0 - t * t) * (c + (3 * c * 0.044715) * u2)
    return value, slope


ROWS = 256


def column_sum(v):
    return jnp.sum(v, axis=0, keepdims=True)


def middle_kernel(
    x, att, w_proj, b_proj, gain, shift, dz, w_up, b_up, w_down, b_down,
    out, dm, d_att, g_proj, sums, g_up, g_bias, g_down,
    middle, a2, a2_t, z, d_a2, h_all, du_all,
):
    step = pl.program_id(0)
    parts = [slice(i, i + ROWS) for i in range(0, x.shape[0], ROWS)]

    @pl.when(step == 0)
    def _():
        for part in parts:
            m = x[part].astype(F32) + (dot(att[part], w_proj[...]) + b_proj[...])
            middle[part] = m
            normal, _ = norm_parts(m)
            a2[part] = (normal * gain[...] + shift[...]).astype(BF16)
        a2_t[...] = a2[...].T
        z[...] = jnp.zeros_like(z)
        d_a2[...] = jnp.zeros_like(d_a2)

    for part in parts:
        u = dot(a2[part], w_up[...]) + b_up[...]
        value, slope = gelu_parts(u)
        h = value.astype(BF16)
        h_all[part] = h
        z[part] += dot(h, w_down[...])
        du = (dot(dz[part], w_down[...], NT) * slope).astype(BF16)
        du_all[part] = du
        d_a2[part] += dot(du, w_up[...], NT)
    du = du_all[...]
    g_bias[...] = column_sum(du.astype(F32))
    g_up[...] = dot(a2_t[...], du).astype(BF16)
    g_down[...] = dot(h_all[...].T, dz[...]).astype(BF16)

    @pl.when(step == pl.num_programs(0) - 1)
    def _():
        total = [jnp.zeros((1, x.shape[1]), F32)] * 4
        for part in parts:
            m = middle[part]
            out[part] = (m + (z[part] + b_down[...])).astype(BF16)
            normal, inv = norm_parts(m)
            grad = d_a2[part]
            scaled = grad * gain[...]
            back = scaled - jnp.mean(scaled, axis=-1, keepdims=True)
            back = back - normal * jnp.mean(scaled * normal, axis=-1, keepdims=True)
            dz32 = dz[part].astype(F32)
            d = dz32 + back * inv
            dm[part] = d
            dy = d.astype(BF16)
            a2[part] = dy
            d_att[part] = dot(dy, w_proj[...], NT).astype(BF16)
            new = [grad * normal, grad, dy.astype(F32), dz32]
            total = [t + column_sum(n) for t, n in zip(total, new)]
        sums[...] = jnp.concatenate(total + total, axis=0)
        g_proj[...] = dot(att[...].T, a2[...]).astype(BF16)


def middle_part(x, att, up_proj, b_proj, gain, shift, dz, b_up, w_down, b_down):
    tokens, width = x.shape
    hidden = b_up.shape[0]
    part = 512
    row = lambda v: v.reshape(1, -1)
    once = lambda shape, col=0: pl.BlockSpec(
        shape, lambda j: (0, col), pipeline_mode=pl.Buffered(1)
    )
    act, vec = once((tokens, width)), once((1, width))
    kept = lambda shape: pl.BlockSpec(shape, lambda j: (0, 0))
    across = pl.BlockSpec((width, part), lambda j: (0, j))
    down = pl.BlockSpec((part, width), lambda j: (j, 0))
    bias = pl.BlockSpec((1, part), lambda j: (0, j))
    return call(
        middle_kernel,
        (hidden // part,),
        [act, act, once((width, width), hidden // width), vec, vec, vec, act]
        + [across, bias, down, vec],
        [kept((tokens, width))] * 3
        + [kept((width, width)), kept((8, width)), across, bias, down],
        [
            jax.ShapeDtypeStruct((tokens, width), BF16),
            jax.ShapeDtypeStruct((tokens, width), F32),
            jax.ShapeDtypeStruct((tokens, width), BF16),
            jax.ShapeDtypeStruct((width, width), BF16),
            jax.ShapeDtypeStruct((8, width), F32),
            jax.ShapeDtypeStruct((width, hidden), BF16),
            jax.ShapeDtypeStruct((1, hidden), F32),
            jax.ShapeDtypeStruct((hidden, width), BF16),
        ],
        12 * tokens * width * hidden,
        "middle_part",
        [
            pltpu.VMEM((tokens, width), F32),
            pltpu.VMEM((tokens, width), BF16),
            pltpu.VMEM((width, tokens), BF16),
            pltpu.VMEM((tokens, width), F32),
            pltpu.VMEM((tokens, width), F32),
            pltpu.VMEM((tokens, part), BF16),
            pltpu.VMEM((tokens, part), BF16),
        ],
    )(
        x, att, up_proj, row(b_proj), row(gain), row(shift), dz,
        up_proj, row(b_up), w_down, row(b_down),
    )


def join_kernel(late, a1, *refs):
    seqs = (len(refs) - 4) // 6
    near, far = refs[: 3 * seqs], refs[3 * seqs : 6 * seqs]
    dp, g, sums, a1_t = refs[6 * seqs :]
    c = pl.program_id(0)
    is_late = late[0] == 1
    is_early = late[0] == 0
    use_keep = (is_late & (c == 0)) | (is_early & (c == 3))
    use_got = (is_late & (c == 1)) | (is_early & ((c == 2) | (c == 4)))
    use_send = is_early & (c == 5)

    @pl.when(c == 0)
    def _():
        a1_t[...] = a1[...].T

    length = near[0].shape[1]
    for b in range(seqs):
        q, k, v = [r[0] for r in near[3 * b : 3 * b + 3]]
        send, keep, got = [r[0] for r in far[3 * b : 3 * b + 3]]
        base = jnp.where(c < 2, q, jnp.where(c < 4, k, v)).astype(F32)
        add = jnp.where(use_keep, keep, jnp.where(use_got, got, send)).astype(F32)
        add = jnp.where(use_keep | use_got | use_send, add, 0.0)
        dp[b * length : (b + 1) * length] = (base + add).astype(BF16)
    whole = dp[...]
    sums[...] = column_sum(whole.astype(F32))
    g[...] = dot(a1_t[...], whole).astype(BF16)


def join(late_ref, a1, near, far):
    tokens, width = a1.shape
    seqs = len(near)
    length, half = near[0][0].shape[1], width // 2
    shape = (1, length, half)
    third = [
        pl.BlockSpec(shape, lambda c, t=t: (0, 0, jnp.clip(c - 2 * t, 0, 1))) for t in range(3)
    ]
    away = [
        pl.BlockSpec(shape, lambda c: (0, 0, 1)),
        pl.BlockSpec(shape, lambda c: (0, 0, 0)),
        pl.BlockSpec(shape, lambda c: (0, 0, jnp.where(c < 3, 0, 1))),
    ]
    return call(
        join_kernel,
        (6,),
        [SCALAR, pl.BlockSpec((tokens, width), lambda c: (0, 0))] + third * seqs + away * seqs,
        [
            pl.BlockSpec((tokens, half), lambda c: (0, c)),
            pl.BlockSpec((width, half), lambda c: (0, c)),
            pl.BlockSpec((1, half), lambda c: (0, c)),
        ],
        [
            jax.ShapeDtypeStruct((tokens, 3 * width), BF16),
            jax.ShapeDtypeStruct((width, 3 * width), BF16),
            jax.ShapeDtypeStruct((1, 3 * width), F32),
        ],
        2 * tokens * width * 3 * width,
        "join",
        [pltpu.VMEM((width, tokens), BF16)],
    )(late_ref, a1, *[r for n in near for r in n], *[r for f in far for r in f])


def tie(value, *others):
    return lax.optimization_barrier((value,) + others)[0]


class Cube:
    def __init__(self):
        self.seq = lax.axis_size("seq")
        self.fsdp = lax.axis_size("fsdp")
        self.count = self.seq * self.fsdp
        self.bits = self.fsdp.bit_length() - 1
        place = lax.axis_index("fsdp")
        seq = lax.axis_index("seq")
        self.me = (seq * self.fsdp + place).astype(jnp.int32).reshape(1)
        self.mine = [seq] + [(place >> (self.bits - 1 - i)) & 1 for i in range(self.bits)]
        self.far = list(range(1, self.bits - 1))
        self.y = self.bits - 1
        self.core = self.bits
        self.x = 0

    def mask(self, dim):
        return self.fsdp if dim == 0 else 1 << (self.bits - dim)

    def swap(self, value, dim):
        if dim == 0:
            return lax.ppermute(value, "seq", [(i, i ^ 1) for i in range(self.seq)])
        flip = self.mask(dim)
        return lax.ppermute(value, "fsdp", [(i, i ^ flip) for i in range(self.fsdp)])


class Gather:
    def __init__(self, cube, block, order):
        self.cube, self.order, self.at = cube, order, 0
        self.value = block[None]

    def step(self, *after):
        other = self.cube.swap(self.value, self.order[self.at])
        if after:
            other = tie(other, *after)
        self.at += 1
        self.value = jnp.concatenate([self.value, other], axis=0)
        return self.value

    def last(self, *after):
        self.other = self.cube.swap(self.value, self.order[self.at])
        if after:
            self.other = tie(self.other, *after)
        return self


def place_kernel(masks, flips, cuts, me, *refs):
    count = len(masks)
    ins, outs = refs[: 2 * count], refs[2 * count :]

    def body(i, carry):
        for source, low, high, target, first in cuts:
            place = me[0]
            for k, mask in enumerate(masks[source]):
                place = place ^ (((i >> k) & 1) * mask)
            for other in range(2):
                outs[target][place ^ (other * flips[source]), :, first : first + high - low] = ins[
                    2 * source + other
                ][i, :, low:high]
        return carry

    lax.fori_loop(0, ins[0].shape[0], body, 0)


def assemble(cube, gathers, cuts, widths, name):
    masks = [[cube.mask(d) for d in g.order[:-1]] for g in gathers]
    flips = [cube.mask(g.order[-1]) for g in gathers]
    rows = gathers[0].value.shape[1]
    args = [item for g in gathers for item in (g.value, g.other)]
    out = pl.pallas_call(
        functools.partial(place_kernel, masks, flips, cuts),
        in_specs=[SCALAR] + [pl.BlockSpec(memory_space=pltpu.VMEM)] * len(args),
        out_specs=[pl.BlockSpec(memory_space=pltpu.VMEM)] * len(widths),
        out_shape=[jax.ShapeDtypeStruct((cube.count, rows, w), BF16) for w in widths],
        compiler_params=pltpu.CompilerParams(vmem_limit_bytes=VMEM),
        cost_estimate=pl.CostEstimate(
            flops=0, bytes_accessed=4 * cube.count * rows * sum(widths), transcendentals=0
        ),
        name=name,
    )(cube.me, *args)
    return [o.reshape(cube.count * rows, -1) for o in out]


class Scatter:
    def __init__(self, cube, whole, order, wire=BF16):
        self.cube, self.order, self.at, self.wire = cube, order, 0, wire
        self.rows, self.tail = whole.shape[0] // cube.count, whole.shape[1:]
        self.value = whole.reshape((2,) * (cube.bits + 1) + (self.rows,) + self.tail)

    def step(self, *after):
        dim = self.order[self.at]
        own = self.cube.mine[dim]
        send = lax.dynamic_index_in_dim(self.value, 1 - own, dim, keepdims=True)
        keep = lax.dynamic_index_in_dim(self.value, own, dim, keepdims=True)
        got = self.cube.swap(send.astype(self.wire), dim)
        if after:
            got = tie(got, *after)
        self.at += 1
        self.value = keep.astype(F32) + got.astype(F32)
        if self.at <= 2:
            self.value = self.value.astype(self.wire)
        return self.value

    def result(self):
        while self.at < len(self.order):
            self.step()
        return self.value.reshape((self.rows,) + self.tail)


def norm_parts(values):
    centre = values - jnp.mean(values, axis=-1, keepdims=True)
    spread_ = jnp.mean(centre * centre, axis=-1, keepdims=True)
    inv = lax.rsqrt(spread_ + EPSILON)
    return centre * inv, inv


def norm_back(grad, normal, inv, gain):
    scaled = grad * gain
    part = scaled - jnp.mean(scaled, axis=-1, keepdims=True)
    part = part - normal * jnp.mean(scaled * normal, axis=-1, keepdims=True)
    return part * inv, jnp.sum(grad * normal, axis=0), jnp.sum(grad, axis=0)


def per_device(
    inputs,
    out_grad,
    first_gain,
    first_shift,
    w_qkv,
    b_query,
    b_value,
    w_proj,
    b_proj,
    second_gain,
    second_shift,
    w_up,
    b_up,
    w_down,
    b_down,
):
    cube = Cube()
    late = lax.axis_index("seq")
    late_ref = late.astype(jnp.int32).reshape(1)
    seqs, length, width = inputs.shape
    tokens = seqs * length
    rows = w_qkv.shape[0]
    half = width // 2
    pairs = width // PAIR

    small = [first_gain, first_shift, b_query, b_value, b_proj, second_gain, second_shift, b_down]
    packed_small = jnp.concatenate(
        [item.reshape(rows, 1) for item in small] + [b_up.reshape(rows, -1)], axis=1
    )
    packed_small = jnp.pad(packed_small, ((0, 0), (0, 128 - packed_small.shape[1])))
    cut = 3 * half
    x_last = cube.far + [cube.y, cube.x, cube.core]
    y_last = cube.far + [cube.x, cube.y, cube.core]
    z_last = [cube.x, cube.y] + cube.far + [cube.core]
    front = Gather(cube, w_qkv[:, :cut], x_last)
    back = Gather(cube, jnp.concatenate([w_qkv[:, cut:], packed_small], axis=1), y_last)
    for _ in cube.far:
        front.step(), back.step()
    gate = (front.value, back.value)
    hidden = w_up.shape[1]
    up_proj = lax.all_gather(
        tie(jnp.concatenate([w_up, w_proj], axis=1), *gate), ("seq", "fsdp"), axis=0, tiled=True
    )
    down_full = lax.all_gather(tie(w_down, *gate), ("seq", "fsdp"), axis=0, tiled=True)
    for _ in range(2):
        front.step(), back.step()
    front.last(), back.last()
    qkv_full, table = assemble(
        cube,
        [front, back],
        [
            (0, 0, cut, 0, 0),
            (1, 0, 3 * width - cut, 0, cut),
            (1, 3 * width - cut, 3 * width - cut + 128, 1, 0),
        ],
        [3 * width, 128],
        "place_qkv",
    )
    table = table.astype(F32)
    (gain_one, shift_one, query_bias, value_bias, proj_bias, gain_two, shift_two, down_bias) = [
        table[:, i] for i in range(8)
    ]
    up_bias = table[:, 8 : 8 + b_up.shape[0] // rows].reshape(-1)

    x = inputs.astype(F32).reshape(tokens, width)
    normal_one, inv_one = norm_parts(x)
    a1 = (normal_one * gain_one + shift_one).astype(BF16)
    bias = jnp.concatenate([query_bias, jnp.zeros((width,), F32), value_bias])
    packed = (dot(a1, qkv_full) + bias).astype(BF16).reshape(seqs, length, 3 * width)

    forth = [(0, 1)]
    back_way = [(1, 0)]
    both_ways = [(0, 1), (1, 0)]
    early = late == 0
    hp = pairs // 2
    tile = 2 * 2 * length * length * PAIR
    whole_shape = jax.ShapeDtypeStruct((1, length, width), BF16)
    half_shape = jax.ShapeDtypeStruct((1, length, half), BF16)
    stat_shape = jax.ShapeDtypeStruct((1, pairs, 2, length), F32)
    half_stat = jax.ShapeDtypeStruct((1, hp, 2, length), F32)
    one, st = cols(length), stats(length)

    def own(b, third, high=0):
        return cols(length, b, third * pairs + high * hp)

    def local_forward(b, data):
        return call(
            local_forward_kernel,
            (pairs,),
            [own(b, 0), own(b, 1), own(b, 2)],
            [one, st],
            [whole_shape, stat_shape],
            tile * pairs,
            f"local_forward_{b}",
        )(data, data, data)

    def cross_forward(b, r):
        return call(
            cross_forward_kernel,
            (hp,),
            [SCALAR, own(b, 0), own(b, 1, 1), own(b, 2, 1), one, cols(length, 0, hp)],
            [one, st],
            [half_shape, half_stat],
            tile * hp,
            f"cross_forward_{b}",
        )(late_ref, packed, packed, packed, r, r)

    def merge(b, o1, l1, o2, l2, o3, l3):
        near, away = (lambda p: jnp.minimum(p, hp - 1)), (lambda p: jnp.maximum(p - hp, 0))
        return call(
            merge_kernel,
            (pairs,),
            [
                SCALAR,
                one,
                st,
                cols(length, low=near),
                stats(length, low=near),
                cols(length, low=away),
                stats(length, low=away),
            ],
            [one, st],
            [whole_shape, stat_shape],
            tile,
            f"merge_{b}",
        )(late_ref, o1, l1, o2, l2, o3, l3)

    arrived, local, cross = [], [], []
    for b in range(seqs):
        row = packed[b : b + 1]
        send = jnp.concatenate(
            [
                jnp.where(early, row[:, :, width : width + half], row[:, :, half:width]),
                row[:, :, 2 * width : 2 * width + half],
            ],
            axis=2,
        )
        arrived.append(lax.ppermute(send, "seq", both_ways))
    data = packed
    for b in range(seqs):
        o1, l1 = local_forward(b, data)
        local.append((o1, l1))
        if b < seqs - 1:
            data = tie(packed, o1)
    for b in range(seqs):
        o2, l2 = cross_forward(b, tie(arrived[b], local[-1][0]))
        o3, l3 = lax.ppermute(o2, "seq", forth), lax.ppermute(l2, "seq", forth)
        cross.append((o2, l2, o3, l3))
    merged = [merge(b, *local[b], *cross[b]) for b in range(seqs)]
    o_flat = jnp.concatenate([m[0] for m in merged], axis=0).reshape(tokens, width)
    stat = [m[1] for m in merged]
    dz = out_grad.reshape(tokens, width)
    outputs, dm, d_att, whole_proj, sums_two, whole_up, sum_up, whole_down = middle_part(
        inputs.reshape(tokens, width),
        o_flat,
        up_proj,
        proj_bias,
        gain_two,
        shift_two,
        dz,
        up_bias,
        down_full,
        down_bias,
    )
    z_first, y_first, x_first = z_last[::-1], y_last[::-1], x_last[::-1]
    grad_down = Scatter(cube, whole_down, z_first)
    grad_up = Scatter(cube, whole_up, y_first)
    grad_proj = Scatter(cube, whole_proj, y_first)
    d_att = d_att.reshape(seqs, length, width)
    delta, rg, rstat, rdelta = [], [], [], []
    for b in range(seqs):
        delta.append(
            call(delta_kernel, (pairs,), [one, cols(length, b)], st, stat_shape, tile, f"delta_{b}")(
                merged[b][0], d_att
            )
        )
        rg.append(lax.ppermute(d_att[b : b + 1, :, half:], "seq", back_way))
    sent = jnp.concatenate([s[:, hp:] for s in stat] + [d[:, hp:] for d in delta], axis=0)
    sent = lax.ppermute(sent, "seq", back_way)
    rstat = [sent[b : b + 1] for b in range(seqs)]
    rdelta = [sent[seqs + b : seqs + b + 1] for b in range(seqs)]
    grad_down.step(*delta), grad_up.step(*delta)

    def local_backward(b, data):
        return call(
            local_backward_kernel,
            (pairs,),
            [own(b, 0), own(b, 1), own(b, 2), cols(length, b), st, st],
            [one, one, one],
            [whole_shape] * 3,
            3 * tile * pairs,
            f"local_backward_{b}",
        )(data, data, data, d_att, stat[b], delta[b])

    def cross_backward(b, r, g):
        return call(
            cross_backward_kernel,
            (hp,),
            [SCALAR, own(b, 0), own(b, 1, 1), own(b, 2, 1), one, cols(length, 0, hp)]
            + [cols(length, b), one, st, st, st, st],
            [pl.BlockSpec((1, length, width), lambda p: (0, 0, 0)), one],
            [whole_shape, half_shape],
            3 * tile * hp,
            f"cross_backward_{b}",
        )(late_ref, packed, packed, packed, r, r, d_att, g, stat[b], delta[b], rstat[b], rdelta[b])

    near_grads, far_grads = [], []
    data = tie(packed, grad_down.value, grad_up.value)
    for b in range(seqs):
        near_grads.append(local_backward(b, data))
        grad_proj.step(near_grads[-1][0])
        if b < seqs - 1:
            data = tie(data, near_grads[-1][0])
    last = near_grads[-1][0]
    grad_down.step(last), grad_up.step(last)
    for b in range(seqs):
        send, keep = cross_backward(b, arrived[b], tie(rg[b], last))
        got = lax.ppermute(send, "seq", both_ways)
        far_grads.append((send, keep, got))
    grad_down.step(send), grad_up.step(send), grad_proj.step(send)
    dp, grad_qkv, sums = join(late_ref, a1, near_grads, far_grads)
    grad_front = Scatter(cube, grad_qkv[:, :cut], x_first)
    grad_back = Scatter(cube, grad_qkv[:, cut:], y_first)
    d_a1 = dot(tie(dp, grad_qkv), qkv_full, NT)
    first_steps = grad_front.step(d_a1), grad_back.step(d_a1)
    second_steps = grad_front.step(), grad_back.step()
    for item in (grad_down, grad_up, grad_proj):
        item.step(*second_steps)
    third_steps = grad_front.step(), grad_back.step()
    for item in (grad_down, grad_up, grad_proj):
        item.at < len(item.order) and item.step(*third_steps)
    input_part, grad_gain_one, grad_shift_one = norm_back(d_a1, normal_one, inv_one, gain_one)
    input_grad = (dm + input_part).reshape(seqs, length, width)

    sums = sums[0]
    grads_small = [
        grad_gain_one,
        grad_shift_one,
        sums[:width],
        sums[2 * width :],
        sums_two[2],
        sums_two[0],
        sums_two[1],
        sums_two[3],
    ]
    devices = width // rows
    pack = jnp.concatenate(
        [item.reshape(devices, rows) for item in grads_small]
        + [sum_up.reshape(devices, -1)],
        axis=1,
    )
    pack = Scatter(cube, pack, x_first, F32).result()[0]
    parts = [pack[i * rows : (i + 1) * rows] for i in range(8)]
    g_up_bias = pack[8 * rows :]
    return (
        outputs.reshape(seqs, length, width),
        input_grad,
        parts[0],
        parts[1],
        jnp.concatenate([grad_front.result(), grad_back.result()], axis=1),
        parts[2],
        parts[3],
        grad_proj.result(),
        parts[4],
        parts[5],
        parts[6],
        grad_up.result(),
        g_up_bias,
        grad_down.result(),
        parts[7],
    )


def solution(mesh):
    vector, matrix = P(("seq", "fsdp")), P(("seq", "fsdp"), None)
    tokens = P("fsdp", "seq", None)
    placed = (
        tokens,
        tokens,
        vector,
        vector,
        matrix,
        vector,
        vector,
        matrix,
        vector,
        vector,
        vector,
        matrix,
        vector,
        matrix,
        vector,
    )
    return jax.shard_map(
        per_device, mesh=mesh, in_specs=placed, out_specs=placed, check_vma=False
    )
```

```python
import functools

import jax
import jax.numpy as jnp
from jax import lax
from jax.experimental import pallas as pl
from jax.experimental.pallas import tpu as pltpu
from jax.sharding import PartitionSpec as P

H = 12
HD = 64
PAIR = 2 * HD
EPSILON = 1e-05
F32 = jnp.float32
BF16 = jnp.bfloat16
NT = (((1,), (1,)), ((), ()))
NN = (((1,), (0,)), ((), ()))
SUB = 256
VMEM = 56 * 1024 * 1024


def dot(a, b, dims=NN):
    return lax.dot_general(a, b, dims, preferred_element_type=F32)


def head_lanes(x, head):
    lane = lax.broadcasted_iota(jnp.int32, x.shape, 1)
    return jnp.where((lane // HD) == head, x, jnp.zeros_like(x))


def masked(scores, start):
    key = lax.broadcasted_iota(jnp.int32, scores.shape, 0)
    query = lax.broadcasted_iota(jnp.int32, scores.shape, 1) + start
    return jnp.where(key <= query, scores, -1e30)


def forward_tile(q, k, v, causal):
    q = q * jnp.asarray(HD**-0.5, q.dtype)
    v_t = v.T
    rows, keys = q.shape[0], k.shape[0]
    outs, stats = [], []
    for head in range(2):
        q_h = head_lanes(q, head)
        v_h = v_t[head * HD : (head + 1) * HD]
        out_h, stat_h = [], []
        for start in range(0, rows, SUB):
            used = start + SUB if causal else keys
            s = dot(k[:used], q_h[start : start + SUB], NT)
            if causal:
                s = masked(s, start)
            top = jnp.max(s, axis=0, keepdims=True)
            e = jnp.exp(s - top)
            total = jnp.sum(e, axis=0, keepdims=True)
            out_h.append(dot(v_h[:, :used], e.astype(BF16)) / total)
            stat_h.append(top + jnp.log(total))
        outs.append(jnp.concatenate(out_h, axis=1))
        stats.append(jnp.concatenate(stat_h, axis=1))
    return jnp.concatenate(outs, axis=0).T, jnp.concatenate(stats, axis=0)


def backward_tile(q, k, v, g, stat, delta, causal):
    q = q * jnp.asarray(HD**-0.5, q.dtype)
    k_t = k.T
    rows, keys = q.shape[0], k.shape[0]
    dq_heads = []
    pieces = [None] * (keys // SUB), [None] * (keys // SUB)

    def add(which, start, value):
        for i in range(value.shape[0] // SUB):
            part = value[i * SUB : (i + 1) * SUB]
            old = pieces[which][start + i]
            pieces[which][start + i] = part if old is None else old + part

    for head in range(2):
        q_h = head_lanes(q, head)
        g_h = head_lanes(g, head)
        k_h = k_t[head * HD : (head + 1) * HD]
        dq_h = []
        for start in range(0, rows, SUB):
            used = start + SUB if causal else keys
            cols = slice(start, start + SUB)
            s = dot(k[:used], q_h[cols], NT)
            if causal:
                s = masked(s, start)
            p = jnp.exp(s - stat[head : head + 1, cols])
            dp = dot(v[:used], g_h[cols], NT)
            ds = (p * (dp - delta[head : head + 1, cols])).astype(BF16)
            add(1, 0, dot(p.astype(BF16), g_h[cols]))
            add(0, 0, dot(ds, q_h[cols]))
            dq_h.append(dot(k_h[:, :used], ds))
        dq_heads.append(jnp.concatenate(dq_h, axis=1))
    dq = jnp.concatenate(dq_heads, axis=0).T * HD**-0.5
    return dq, jnp.concatenate(pieces[0], axis=0), jnp.concatenate(pieces[1], axis=0)


def local_forward_kernel(q, k, v, o, stat):
    out, lse = forward_tile(q[0], k[0], v[0], True)
    o[0] = out.astype(BF16)
    stat[0, 0] = lse


def cross_forward_kernel(late, q, k, v, r1, r2, o, stat):
    is_late = late[0] == 1
    r = r1[0]
    out, lse = forward_tile(
        jnp.where(is_late, q[0], r),
        jnp.where(is_late, r, k[0]),
        jnp.where(is_late, r2[0], v[0]),
        False,
    )
    o[0] = out.astype(BF16)
    stat[0, 0] = lse


def spread(rows, size):
    a = jnp.broadcast_to(rows[0:1], (HD, size))
    b = jnp.broadcast_to(rows[1:2], (HD, size))
    return jnp.concatenate([a, b], axis=0).T


def merge_kernel(late, *refs):
    o, stat = refs[-2:]
    seqs, pairs = stat.shape[:2]
    is_late = late[0] == 1
    for b in range(seqs):
        o1, l1, o2, l2, o3, l3 = refs[6 * b : 6 * b + 6]
        for p in range(pairs):
            near = p < pairs // 2
            at = p if near else p - pairs // 2
            here = slice(p * PAIR, (p + 1) * PAIR)
            there = slice(at * PAIR, (at + 1) * PAIR)
            first = l1[0, p]
            second = (l2 if near else l3)[0, at]
            gap = second - first
            weight = jnp.where(is_late, 1.0 / (1.0 + jnp.exp(-gap)), 0.0)
            both = jnp.maximum(first, second) + jnp.log(1.0 + jnp.exp(-jnp.abs(gap)))
            stat[b, p] = jnp.where(is_late, both, first)
            own = o1[0, :, here].astype(F32)
            other = (o2 if near else o3)[0, :, there].astype(F32)
            o[b, :, here] = (own + spread(weight, own.shape[0]) * (other - own)).astype(BF16)


def local_backward_kernel(q, k, v, g, stat, delta, dq, dk, dv):
    a, b, c = backward_tile(q[0], k[0], v[0], g[0], stat[0, 0], delta[0, 0], True)
    dq[0] = a.astype(BF16)
    dk[0] = b.astype(BF16)
    dv[0] = c.astype(BF16)


def cross_backward_kernel(
    late, q, k, v, r1, r2, g, rg, stat, delta, rstat, rdelta, send, keep
):
    is_late = late[0] == 1
    r = r1[0]
    a, b, c = backward_tile(
        jnp.where(is_late, q[0], r),
        jnp.where(is_late, r, k[0]),
        jnp.where(is_late, r2[0], v[0]),
        jnp.where(is_late, g[0], rg[0]),
        jnp.where(is_late, stat[0, 0], rstat[0, 0, 0]),
        jnp.where(is_late, delta[0, 0], rdelta[0, 0, 0]),
        False,
    )
    a, b = a.astype(BF16), b.astype(BF16)
    place = pl.program_id(0) * PAIR
    span = pl.num_programs(0) * PAIR
    send[0, :, pl.ds(pl.multiple_of(place, PAIR), PAIR)] = jnp.where(is_late, b, a)
    send[0, :, pl.ds(pl.multiple_of(span + place, PAIR), PAIR)] = c.astype(BF16)
    keep[0] = jnp.where(is_late, a, b)


def cols(length, b0=0, shift=0, low=lambda p: p):
    return pl.BlockSpec((1, length, PAIR), lambda p: (b0, 0, low(p) + shift))


def stats(length, shift=0, low=lambda p: p):
    return pl.BlockSpec((1, 1, 2, length), lambda p: (0, low(p) + shift, 0, 0))


SCALAR = pl.BlockSpec(memory_space=pltpu.SMEM)


def skip(kernel, count, *refs):
    kernel(*refs[count:])


def call(kernel, grid, ins, outs, shapes, cost, name, scratch=(), after=()):
    body = functools.partial(skip, kernel, len(after)) if after else kernel
    made = pl.pallas_call(
        body,
        grid=grid,
        in_specs=[pl.BlockSpec(memory_space=pl.ANY)] * len(after) + list(ins),
        out_specs=outs,
        out_shape=shapes,
        scratch_shapes=scratch,
        compiler_params=pltpu.CompilerParams(vmem_limit_bytes=VMEM),
        cost_estimate=pl.CostEstimate(
            flops=cost, bytes_accessed=cost // 256, transcendentals=cost // 256
        ),
        name=name,
    )
    return functools.partial(made, *after)


def gelu_parts(u):
    c = (2.0 / jnp.pi) ** 0.5
    u2 = u * u
    t = jnp.tanh(u * (c + (c * 0.044715) * u2))
    half = 0.5 + 0.5 * t
    value = u * half
    slope = half + 0.5 * u * (1.0 - t * t) * (c + (3 * c * 0.044715) * u2)
    return value, slope


ROWS = 256


def column_sum(v):
    return jnp.sum(v, axis=0, keepdims=True)


def middle_kernel(
    x, att, w_proj, b_proj, gain, shift, dz, w_up, b_up, w_down, b_down,
    out, dm, d_att, delta, sums, g_across, g_bias, g_down,
    middle, a2, a2_t, z, d_a2, h_all, du_all,
):
    step = pl.program_id(0)
    last = pl.num_programs(0) - 1
    parts = [slice(i, i + ROWS) for i in range(0, x.shape[0], ROWS)]

    @pl.when(step == 0)
    def _():
        for part in parts:
            m = x[part].astype(F32) + (dot(att[part], w_proj[...]) + b_proj[...])
            middle[part] = m
            normal, _ = norm_parts(m)
            a2[part] = (normal * gain[...] + shift[...]).astype(BF16)
        a2_t[...] = a2[...].T
        z[...] = jnp.zeros_like(z)
        d_a2[...] = jnp.zeros_like(d_a2)

    @pl.when(step < last)
    def _():
        for part in parts:
            u = dot(a2[part], w_up[...]) + b_up[...]
            value, slope = gelu_parts(u)
            h = value.astype(BF16)
            h_all[part] = h
            z[part] += dot(h, w_down[...])
            du = (dot(dz[part], w_down[...], NT) * slope).astype(BF16)
            du_all[part] = du
            d_a2[part] += dot(du, w_up[...], NT)
        du = du_all[...]
        g_bias[...] = column_sum(du.astype(F32))
        g_across[...] = dot(a2_t[...], du).astype(BF16)
        g_down[...] = dot(h_all[...].T, dz[...]).astype(BF16)

    @pl.when(step == last)
    def _():
        total = [jnp.zeros((1, x.shape[1]), F32)] * 4
        length = delta.shape[-1]
        for part in parts:
            m = middle[part]
            out[part] = (m + (z[part] + b_down[...])).astype(BF16)
            normal, inv = norm_parts(m)
            grad = d_a2[part]
            scaled = grad * gain[...]
            back = scaled - jnp.mean(scaled, axis=-1, keepdims=True)
            back = back - normal * jnp.mean(scaled * normal, axis=-1, keepdims=True)
            dz32 = dz[part].astype(F32)
            d = dz32 + back * inv
            dm[part] = d
            dy = d.astype(BF16)
            a2[part] = dy
            d_o = dot(dy, w_proj[...], NT).astype(BF16)
            d_att[part] = d_o
            prod = (d_o.astype(F32) * att[part].astype(F32)).T
            b, first = divmod(part.start, length)
            for p in range(delta.shape[1]):
                heads = [prod[i * HD : (i + 1) * HD] for i in (2 * p, 2 * p + 1)]
                delta[b, p, :, first : first + ROWS] = jnp.concatenate(
                    [column_sum(h) for h in heads], axis=0
                )
            new = [grad * normal, grad, dy.astype(F32), dz32]
            total = [t + column_sum(n) for t, n in zip(total, new)]
        sums[...] = jnp.concatenate(total + total, axis=0)
        g_across[...] = dot(att[...].T, a2[...]).astype(BF16)


def middle_part(x, att, up_proj, b_proj, gain, shift, dz, b_up, w_down, b_down, seqs):
    tokens, width = x.shape
    hidden = b_up.shape[0]
    part = width
    steps = hidden // part
    row = lambda v: v.reshape(1, -1)
    once = lambda shape, col=0: pl.BlockSpec(
        shape, lambda j: (0, col), pipeline_mode=pl.Buffered(1)
    )
    act, vec = once((tokens, width)), once((1, width))
    kept = lambda shape: pl.BlockSpec(shape, lambda j: (0,) * len(shape))
    at = lambda j: jnp.minimum(j, steps - 1)
    across = pl.BlockSpec((width, part), lambda j: (0, at(j)))
    down = pl.BlockSpec((part, width), lambda j: (at(j), 0))
    bias = pl.BlockSpec((1, part), lambda j: (0, at(j)))
    delta = (seqs, width // PAIR, 2, tokens // seqs)
    return call(
        middle_kernel,
        (steps + 1,),
        [act, act, once((width, width), steps), vec, vec, vec, act]
        + [across, bias, down, vec],
        [kept((tokens, width))] * 3
        + [kept(delta), kept((8, width))]
        + [pl.BlockSpec((width, part), lambda j: (0, j)), bias, down],
        [
            jax.ShapeDtypeStruct((tokens, width), BF16),
            jax.ShapeDtypeStruct((tokens, width), F32),
            jax.ShapeDtypeStruct((tokens, width), BF16),
            jax.ShapeDtypeStruct(delta, F32),
            jax.ShapeDtypeStruct((8, width), F32),
            jax.ShapeDtypeStruct((width, hidden + width), BF16),
            jax.ShapeDtypeStruct((1, hidden), F32),
            jax.ShapeDtypeStruct((hidden, width), BF16),
        ],
        12 * tokens * width * hidden,
        "middle_part",
        [
            pltpu.VMEM((tokens, width), F32),
            pltpu.VMEM((tokens, width), BF16),
            pltpu.VMEM((width, tokens), BF16),
            pltpu.VMEM((tokens, width), F32),
            pltpu.VMEM((tokens, width), F32),
            pltpu.VMEM((tokens, part), BF16),
            pltpu.VMEM((tokens, part), BF16),
        ],
    )(
        x, att, up_proj, row(b_proj), row(gain), row(shift), dz,
        up_proj, row(b_up), w_down, row(b_down),
    )


def join_kernel(first, late, a1, *refs):
    seqs = (len(refs) - 4) // 6
    near, far = refs[: 3 * seqs], refs[3 * seqs : 6 * seqs]
    dp, g, sums, a1_t = refs[6 * seqs :]
    c = pl.program_id(0) + first
    is_late = late[0] == 1
    is_early = late[0] == 0
    use_keep = (is_late & (c == 0)) | (is_early & (c == 3))
    use_got = (is_late & (c == 1)) | (is_early & ((c == 2) | (c == 4)))
    use_send = is_early & (c == 5)

    @pl.when(c == first)
    def _():
        a1_t[...] = a1[...].T

    length = near[0].shape[1]
    for b in range(seqs):
        q, k, v = [r[0] for r in near[3 * b : 3 * b + 3]]
        send, keep, got = [r[0] for r in far[3 * b : 3 * b + 3]]
        base = jnp.where(c < 2, q, jnp.where(c < 4, k, v)).astype(F32)
        add = jnp.where(use_keep, keep, jnp.where(use_got, got, send)).astype(F32)
        add = jnp.where(use_keep | use_got | use_send, add, 0.0)
        dp[b * length : (b + 1) * length] = (base + add).astype(BF16)
    whole = dp[...]
    sums[...] = column_sum(whole.astype(F32))
    g[...] = dot(a1_t[...], whole).astype(BF16)


def join(late_ref, a1, near, far, first, count, after):
    tokens, width = a1.shape
    seqs = len(near)
    length, half = near[0][0].shape[1], width // 2
    shape = (1, length, half)
    third = [
        pl.BlockSpec(shape, lambda c, t=t: (0, 0, jnp.clip(c + first - 2 * t, 0, 1))) for t in range(3)
    ]
    away = [
        pl.BlockSpec(shape, lambda c: (0, 0, 1)),
        pl.BlockSpec(shape, lambda c: (0, 0, 0)),
        pl.BlockSpec(shape, lambda c: (0, 0, jnp.where(c + first < 3, 0, 1))),
    ]
    return call(
        functools.partial(join_kernel, first),
        (count,),
        [SCALAR, pl.BlockSpec((tokens, width), lambda c: (0, 0))] + third * seqs + away * seqs,
        [
            pl.BlockSpec((tokens, half), lambda c: (0, c)),
            pl.BlockSpec((width, half), lambda c: (0, c)),
            pl.BlockSpec((1, half), lambda c: (0, c)),
        ],
        [
            jax.ShapeDtypeStruct((tokens, count * half), BF16),
            jax.ShapeDtypeStruct((width, count * half), BF16),
            jax.ShapeDtypeStruct((1, count * half), F32),
        ],
        2 * tokens * width * count * half,
        f"join_{first}",
        [pltpu.VMEM((width, tokens), BF16)],
        after,
    )(late_ref, a1, *[r for n in near for r in n], *[r for f in far for r in f])


def nothing(*refs):
    pass


def tie(value, *others):
    anywhere = pl.BlockSpec(memory_space=pl.ANY)
    return pl.pallas_call(
        nothing,
        in_specs=[anywhere] * (1 + len(others)),
        out_specs=anywhere,
        out_shape=jax.ShapeDtypeStruct(value.shape, value.dtype),
        input_output_aliases={0: 0},
        name="tie",
    )(value, *others)


class Cube:
    def __init__(self):
        self.seq = lax.axis_size("seq")
        self.fsdp = lax.axis_size("fsdp")
        self.count = self.seq * self.fsdp
        self.bits = self.fsdp.bit_length() - 1
        place = lax.axis_index("fsdp")
        seq = lax.axis_index("seq")
        self.me = (seq * self.fsdp + place).astype(jnp.int32).reshape(1)
        self.mine = [seq] + [(place >> (self.bits - 1 - i)) & 1 for i in range(self.bits)]
        self.far = list(range(1, self.bits - 1))
        self.y = self.bits - 1
        self.core = self.bits
        self.x = 0

    def mask(self, dim):
        return self.fsdp if dim == 0 else 1 << (self.bits - dim)

    def swap(self, value, dim):
        if dim == 0:
            return lax.ppermute(value, "seq", [(i, i ^ 1) for i in range(self.seq)])
        flip = self.mask(dim)
        return lax.ppermute(value, "fsdp", [(i, i ^ flip) for i in range(self.fsdp)])


class Gather:
    def __init__(self, cube, block, order):
        self.cube, self.order, self.at = cube, order, 0
        self.value = block[None]

    def step(self, *after):
        other = self.cube.swap(self.value, self.order[self.at])
        if after:
            other = tie(other, *after)
        self.at += 1
        self.value = jnp.concatenate([self.value, other], axis=0)
        return self.value

    def last(self, *after):
        self.other = self.cube.swap(self.value, self.order[self.at])
        if after:
            self.other = tie(self.other, *after)
        return self


def place_kernel(masks, flips, cuts, me, *refs):
    count = len(masks)
    ins, outs = refs[: 2 * count], refs[2 * count :]

    def body(i, carry):
        for source, low, high, target, first in cuts:
            place = me[0]
            for k, mask in enumerate(masks[source]):
                place = place ^ (((i >> k) & 1) * mask)
            for other in range(2):
                outs[target][place ^ (other * flips[source]), :, first : first + high - low] = ins[
                    2 * source + other
                ][i, :, low:high]
        return carry

    lax.fori_loop(0, ins[0].shape[0], body, 0)


def assemble(cube, gathers, cuts, widths, name):
    masks = [[cube.mask(d) for d in g.order[:-1]] for g in gathers]
    flips = [cube.mask(g.order[-1]) for g in gathers]
    rows = gathers[0].value.shape[1]
    args = [item for g in gathers for item in (g.value, g.other)]
    out = pl.pallas_call(
        functools.partial(place_kernel, masks, flips, cuts),
        in_specs=[SCALAR] + [pl.BlockSpec(memory_space=pltpu.VMEM)] * len(args),
        out_specs=[pl.BlockSpec(memory_space=pltpu.VMEM)] * len(widths),
        out_shape=[jax.ShapeDtypeStruct((cube.count, rows, w), BF16) for w in widths],
        compiler_params=pltpu.CompilerParams(vmem_limit_bytes=VMEM),
        cost_estimate=pl.CostEstimate(
            flops=0, bytes_accessed=4 * cube.count * rows * sum(widths), transcendentals=0
        ),
        name=name,
    )(cube.me, *args)
    return [o.reshape(cube.count * rows, -1) for o in out]


class Scatter:
    def __init__(self, cube, whole, order, wire=BF16):
        self.cube, self.order, self.at, self.wire = cube, order, 0, wire
        self.rows, self.tail = whole.shape[0] // cube.count, whole.shape[1:]
        self.value = whole.reshape((2,) * (cube.bits + 1) + (self.rows,) + self.tail)
        self.send()

    def send(self):
        dim = self.order[self.at]
        own = self.cube.mine[dim]
        sent = lax.dynamic_index_in_dim(self.value, 1 - own, dim, keepdims=True)
        self.sent = sent.astype(self.wire)
        self.got = self.cube.swap(self.sent, dim)

    def step(self, *after):
        if self.at == len(self.order):
            return self.value
        dim = self.order[self.at]
        got = tie(self.got, *after) if after else self.got
        keep = lax.dynamic_index_in_dim(self.value, self.cube.mine[dim], dim, keepdims=True)
        self.at += 1
        self.value = keep.astype(F32) + got.astype(F32)
        if self.at <= 2:
            self.value = self.value.astype(self.wire)
        if self.at < len(self.order):
            self.send()
        else:
            self.sent = self.value
        return self.sent

    def result(self):
        while self.at < len(self.order):
            self.step()
        return self.value.reshape((self.rows,) + self.tail)


def norm_parts(values):
    centre = values - jnp.mean(values, axis=-1, keepdims=True)
    spread_ = jnp.mean(centre * centre, axis=-1, keepdims=True)
    inv = lax.rsqrt(spread_ + EPSILON)
    return centre * inv, inv


def norm_back(grad, normal, inv, gain):
    scaled = grad * gain
    part = scaled - jnp.mean(scaled, axis=-1, keepdims=True)
    part = part - normal * jnp.mean(scaled * normal, axis=-1, keepdims=True)
    return part * inv, jnp.sum(grad * normal, axis=0), jnp.sum(grad, axis=0)


def per_device(
    inputs,
    out_grad,
    first_gain,
    first_shift,
    w_qkv,
    b_query,
    b_value,
    w_proj,
    b_proj,
    second_gain,
    second_shift,
    w_up,
    b_up,
    w_down,
    b_down,
):
    cube = Cube()
    late = lax.axis_index("seq")
    late_ref = late.astype(jnp.int32).reshape(1)
    seqs, length, width = inputs.shape
    tokens = seqs * length
    rows = w_qkv.shape[0]
    half = width // 2
    pairs = width // PAIR

    small = [first_gain, first_shift, b_query, b_value, b_proj, second_gain, second_shift, b_down]
    packed_small = jnp.concatenate(
        [item.reshape(rows, 1) for item in small] + [b_up.reshape(rows, -1)], axis=1
    )
    packed_small = jnp.pad(packed_small, ((0, 0), (0, 128 - packed_small.shape[1])))
    cut = 3 * half
    x_last = cube.far + [cube.y, cube.x, cube.core]
    y_last = cube.far + [cube.x, cube.y, cube.core]
    front = Gather(cube, w_qkv[:, :cut], x_last)
    back = Gather(cube, jnp.concatenate([w_qkv[:, cut:], packed_small], axis=1), y_last)
    hidden = w_up.shape[1]
    up_proj = lax.all_gather(
        jnp.concatenate([w_up, w_proj], axis=1), ("seq", "fsdp"), axis=0, tiled=True
    )
    down_full = lax.all_gather(w_down, ("seq", "fsdp"), axis=0, tiled=True)
    for _ in x_last[:-1]:
        front.step(), back.step()
    front.last(), back.last()
    qkv_full, table = assemble(
        cube,
        [front, back],
        [
            (0, 0, cut, 0, 0),
            (1, 0, 3 * width - cut, 0, cut),
            (1, 3 * width - cut, 3 * width - cut + 128, 1, 0),
        ],
        [3 * width, 128],
        "place_qkv",
    )
    table = table.astype(F32)
    (gain_one, shift_one, query_bias, value_bias, proj_bias, gain_two, shift_two, down_bias) = [
        table[:, i] for i in range(8)
    ]
    up_bias = table[:, 8 : 8 + b_up.shape[0] // rows].reshape(-1)

    x = inputs.astype(F32).reshape(tokens, width)
    normal_one, inv_one = norm_parts(x)
    a1 = (normal_one * gain_one + shift_one).astype(BF16)
    bias = jnp.concatenate([query_bias, jnp.zeros((width,), F32), value_bias])
    packed = (dot(a1, qkv_full) + bias).astype(BF16).reshape(seqs, length, 3 * width)

    forth = [(0, 1)]
    back_way = [(1, 0)]
    both_ways = [(0, 1), (1, 0)]
    early = late == 0
    hp = pairs // 2
    tile = 2 * 2 * length * length * PAIR
    whole_shape = jax.ShapeDtypeStruct((1, length, width), BF16)
    half_shape = jax.ShapeDtypeStruct((1, length, half), BF16)
    stat_shape = jax.ShapeDtypeStruct((1, pairs, 2, length), F32)
    half_stat = jax.ShapeDtypeStruct((1, hp, 2, length), F32)
    one, st = cols(length), stats(length)

    def own(b, third, high=0):
        return cols(length, b, third * pairs + high * hp)

    def local_forward(b, data):
        return call(
            local_forward_kernel,
            (pairs,),
            [own(b, 0), own(b, 1), own(b, 2)],
            [one, st],
            [whole_shape, stat_shape],
            tile * pairs,
            f"local_forward_{b}",
        )(data, data, data)

    def cross_forward(b, r, after):
        return call(
            cross_forward_kernel,
            (hp,),
            [SCALAR, own(b, 0), own(b, 1, 1), own(b, 2, 1), one, cols(length, 0, hp)],
            [one, st],
            [half_shape, half_stat],
            tile * hp,
            f"cross_forward_{b}",
            after=after,
        )(late_ref, packed, packed, packed, r, r)

    arrived, local, cross = [], [], []
    for b in range(seqs):
        row = packed[b : b + 1]
        send = jnp.concatenate(
            [
                jnp.where(early, row[:, :, width : width + half], row[:, :, half:width]),
                row[:, :, 2 * width : 2 * width + half],
            ],
            axis=2,
        )
        arrived.append(lax.ppermute(send, "seq", both_ways))
    for b in range(seqs):
        local.append(local_forward(b, packed))
    after = (local[-1][0],)
    for b in range(seqs):
        o2, l2 = cross_forward(b, arrived[b], after)
        after = (o2,)
        o3, l3 = lax.ppermute(o2, "seq", forth), lax.ppermute(l2, "seq", forth)
        cross.append((o2, l2, o3, l3))
    flat = [item for b in range(seqs) for item in local[b] + cross[b]]
    attended, stat_all = pl.pallas_call(
        merge_kernel,
        in_specs=[SCALAR] + [pl.BlockSpec(memory_space=pltpu.VMEM)] * len(flat),
        out_specs=[pl.BlockSpec(memory_space=pltpu.VMEM)] * 2,
        out_shape=[
            jax.ShapeDtypeStruct((seqs, length, width), BF16),
            jax.ShapeDtypeStruct((seqs, pairs, 2, length), F32),
        ],
        compiler_params=pltpu.CompilerParams(vmem_limit_bytes=VMEM),
        name="merge",
    )(late_ref, *flat)
    o_flat = attended.reshape(tokens, width)
    dz = out_grad.reshape(tokens, width)
    outputs, dm, d_att, delta_all, sums_two, whole_across, sum_up, whole_down = middle_part(
        inputs.reshape(tokens, width),
        o_flat,
        up_proj,
        proj_bias,
        gain_two,
        shift_two,
        dz,
        up_bias,
        down_full,
        down_bias,
        seqs,
    )
    y_first, x_first = y_last[::-1], x_last[::-1]
    mixed = [cube.core] + cube.far[-1:] + [cube.y] + cube.far[:-1][::-1] + [cube.x]
    grad_down = Scatter(cube, whole_down, mixed)
    grad_across = Scatter(cube, whole_across, y_first)
    d_att = d_att.reshape(seqs, length, width)
    rg = [lax.ppermute(d_att[b : b + 1, :, half:], "seq", back_way) for b in range(seqs)]
    sent = jnp.stack([stat_all[:, hp:], delta_all[:, hp:]])
    sent = lax.ppermute(sent, "seq", back_way)
    st_of = lambda b: pl.BlockSpec((1, 1, 2, length), lambda p: (b, p, 0, 0))
    far_of = lambda i, b: pl.BlockSpec((1, 1, 1, 2, length), lambda p: (i, b, p, 0, 0))
    def local_backward(b, after):
        return call(
            local_backward_kernel,
            (pairs,),
            [own(b, 0), own(b, 1), own(b, 2), cols(length, b), st_of(b), st_of(b)],
            [one, one, one],
            [whole_shape] * 3,
            3 * tile * pairs,
            f"local_backward_{b}",
            after=after,
        )(packed, packed, packed, d_att, stat_all, delta_all)

    def cross_backward(b, r, g, after):
        return call(
            cross_backward_kernel,
            (hp,),
            [SCALAR, own(b, 0), own(b, 1, 1), own(b, 2, 1), one, cols(length, 0, hp)]
            + [cols(length, b), one, st_of(b), st_of(b), far_of(0, b), far_of(1, b)],
            [pl.BlockSpec((1, length, width), lambda p: (0, 0, 0)), one],
            [whole_shape, half_shape],
            3 * tile * hp,
            f"cross_backward_{b}",
            after=after,
        )(late_ref, packed, packed, packed, r, r, d_att, g, stat_all, delta_all, sent, sent)

    near_grads, far_grads = [], []
    after = (grad_down.sent, grad_across.sent)
    for b in range(seqs):
        near_grads.append(local_backward(b, after))
        moved = ()
        if b == 0:
            moved = grad_down.step(), grad_across.step()
        send, keep = cross_backward(b, arrived[b], rg[b], (near_grads[b][0],))
        far_grads.append((send, keep, lax.ppermute(send, "seq", both_ways)))
        after = (send,) + moved
    grad_down.step(), grad_across.step()
    dp_front, g_front, sums_front = join(late_ref, a1, near_grads, far_grads, 0, 3, ())
    grad_front = Scatter(cube, g_front, x_first)
    moved = grad_front.step()
    dp_back, g_back, sums_back = join(late_ref, a1, near_grads, far_grads, 3, 3, (moved,))
    grad_back = Scatter(cube, g_back, y_first)
    moved = grad_down.step(grad_back.sent), grad_across.step(grad_back.sent)
    moved = (grad_back.step(*moved),) + moved
    dp_back = tie(dp_back, *moved)
    d_a1 = dot(dp_front, qkv_full[:, :cut], NT) + dot(dp_back, qkv_full[:, cut:], NT)
    moved = grad_front.step(d_a1), grad_back.step(d_a1)
    moved = grad_down.step(*moved), grad_across.step(*moved)
    moved = grad_front.step(*moved), grad_back.step(*moved)
    sums = jnp.concatenate([sums_front[0], sums_back[0]])
    input_part, grad_gain_one, grad_shift_one = norm_back(d_a1, normal_one, inv_one, gain_one)
    input_grad = (dm + input_part).reshape(seqs, length, width)

    grads_small = [
        grad_gain_one,
        grad_shift_one,
        sums[:width],
        sums[2 * width :],
        sums_two[2],
        sums_two[0],
        sums_two[1],
        sums_two[3],
    ]
    devices = width // rows
    pack = jnp.concatenate(
        [item.reshape(devices, rows) for item in grads_small]
        + [sum_up.reshape(devices, -1)],
        axis=1,
    )
    pack = lax.all_to_all(pack, ("seq", "fsdp"), split_axis=0, concat_axis=0, tiled=True)
    pack = jnp.sum(pack, axis=0)
    parts = [pack[i * rows : (i + 1) * rows] for i in range(8)]
    g_up_bias = pack[8 * rows :]
    across = grad_across.result()
    return (
        outputs.reshape(seqs, length, width),
        input_grad,
        parts[0],
        parts[1],
        jnp.concatenate([grad_front.result(), grad_back.result()], axis=1),
        parts[2],
        parts[3],
        across[:, hidden:],
        parts[4],
        parts[5],
        parts[6],
        across[:, :hidden],
        g_up_bias,
        grad_down.result(),
        parts[7],
    )


def solution(mesh):
    vector, matrix = P(("seq", "fsdp")), P(("seq", "fsdp"), None)
    tokens = P("fsdp", "seq", None)
    placed = (
        tokens,
        tokens,
        vector,
        vector,
        matrix,
        vector,
        vector,
        matrix,
        vector,
        vector,
        vector,
        matrix,
        vector,
        matrix,
        vector,
    )
    return jax.shard_map(
        per_device, mesh=mesh, in_specs=placed, out_specs=placed, check_vma=False
    )
```

```python
import functools

import jax
import jax.numpy as jnp
from jax import lax
from jax.experimental import pallas as pl
from jax.experimental.pallas import tpu as pltpu
from jax.sharding import PartitionSpec as P

H = 12
HD = 64
PAIR = 2 * HD
EPSILON = 1e-05
F32 = jnp.float32
BF16 = jnp.bfloat16
NT = (((1,), (1,)), ((), ()))
NN = (((1,), (0,)), ((), ()))
SUB = 256
VMEM = 56 * 1024 * 1024


def dot(a, b, dims=NN):
    return lax.dot_general(a, b, dims, preferred_element_type=F32)


def head_lanes(x, head):
    lane = lax.broadcasted_iota(jnp.int32, x.shape, 1)
    return jnp.where((lane // HD) == head, x, jnp.zeros_like(x))


def masked(scores, start):
    key = lax.broadcasted_iota(jnp.int32, scores.shape, 0)
    query = lax.broadcasted_iota(jnp.int32, scores.shape, 1) + start
    return jnp.where(key <= query, scores, -1e30)


def forward_tile(q, k, v, causal):
    q = q * jnp.asarray(HD**-0.5, q.dtype)
    v_t = v.T
    rows, keys = q.shape[0], k.shape[0]
    outs, stats = [], []
    for head in range(2):
        q_h = head_lanes(q, head)
        v_h = v_t[head * HD : (head + 1) * HD]
        out_h, stat_h = [], []
        for start in range(0, rows, SUB):
            used = start + SUB if causal else keys
            s = dot(k[:used], q_h[start : start + SUB], NT)
            if causal:
                s = masked(s, start)
            top = jnp.max(s, axis=0, keepdims=True)
            e = jnp.exp(s - top)
            total = jnp.sum(e, axis=0, keepdims=True)
            out_h.append(dot(v_h[:, :used], e.astype(BF16)) / total)
            stat_h.append(top + jnp.log(total))
        outs.append(jnp.concatenate(out_h, axis=1))
        stats.append(jnp.concatenate(stat_h, axis=1))
    return jnp.concatenate(outs, axis=0).T, jnp.concatenate(stats, axis=0)


def backward_tile(q, k, v, g, stat, delta, causal):
    q = q * jnp.asarray(HD**-0.5, q.dtype)
    k_t = k.T
    rows, keys = q.shape[0], k.shape[0]
    dq_heads = []
    pieces = [None] * (keys // SUB), [None] * (keys // SUB)

    def add(which, start, value):
        for i in range(value.shape[0] // SUB):
            part = value[i * SUB : (i + 1) * SUB]
            old = pieces[which][start + i]
            pieces[which][start + i] = part if old is None else old + part

    for head in range(2):
        q_h = head_lanes(q, head)
        g_h = head_lanes(g, head)
        k_h = k_t[head * HD : (head + 1) * HD]
        dq_h = []
        for start in range(0, rows, SUB):
            used = start + SUB if causal else keys
            cols = slice(start, start + SUB)
            s = dot(k[:used], q_h[cols], NT)
            if causal:
                s = masked(s, start)
            p = jnp.exp(s - stat[head : head + 1, cols])
            dp = dot(v[:used], g_h[cols], NT)
            ds = (p * (dp - delta[head : head + 1, cols])).astype(BF16)
            add(1, 0, dot(p.astype(BF16), g_h[cols]))
            add(0, 0, dot(ds, q_h[cols]))
            dq_h.append(dot(k_h[:, :used], ds))
        dq_heads.append(jnp.concatenate(dq_h, axis=1))
    dq = jnp.concatenate(dq_heads, axis=0).T * HD**-0.5
    return dq, jnp.concatenate(pieces[0], axis=0), jnp.concatenate(pieces[1], axis=0)


def local_forward_kernel(q, k, v, o, stat):
    out, lse = forward_tile(q[0], k[0], v[0], True)
    o[0] = out.astype(BF16)
    stat[0, 0] = lse


def cross_forward_kernel(late, q, k, v, r1, r2, o, stat):
    is_late = late[0] == 1
    r = r1[0]
    out, lse = forward_tile(
        jnp.where(is_late, q[0], r),
        jnp.where(is_late, r, k[0]),
        jnp.where(is_late, r2[0], v[0]),
        False,
    )
    o[0] = out.astype(BF16)
    stat[0, 0] = lse


def spread(rows, size):
    a = jnp.broadcast_to(rows[0:1], (HD, size))
    b = jnp.broadcast_to(rows[1:2], (HD, size))
    return jnp.concatenate([a, b], axis=0).T


def merge_kernel(late, *refs):
    o, stat = refs[-2:]
    seqs, pairs = stat.shape[:2]
    is_late = late[0] == 1
    for b in range(seqs):
        o1, l1, o2, l2, o3, l3 = refs[6 * b : 6 * b + 6]
        for p in range(pairs):
            near = p < pairs // 2
            at = p if near else p - pairs // 2
            here = slice(p * PAIR, (p + 1) * PAIR)
            there = slice(at * PAIR, (at + 1) * PAIR)
            first = l1[0, p]
            second = (l2 if near else l3)[0, at]
            gap = second - first
            weight = jnp.where(is_late, 1.0 / (1.0 + jnp.exp(-gap)), 0.0)
            both = jnp.maximum(first, second) + jnp.log(1.0 + jnp.exp(-jnp.abs(gap)))
            stat[b, p] = jnp.where(is_late, both, first)
            own = o1[0, :, here].astype(F32)
            other = (o2 if near else o3)[0, :, there].astype(F32)
            o[b, :, here] = (own + spread(weight, own.shape[0]) * (other - own)).astype(BF16)


def local_backward_kernel(q, k, v, g, stat, delta, dq, dk, dv):
    a, b, c = backward_tile(q[0], k[0], v[0], g[0], stat[0, 0], delta[0, 0], True)
    dq[0] = a.astype(BF16)
    dk[0] = b.astype(BF16)
    dv[0] = c.astype(BF16)


def cross_backward_kernel(
    late, q, k, v, r1, r2, g, rg, stat, delta, rstat, rdelta, send, keep
):
    is_late = late[0] == 1
    r = r1[0]
    a, b, c = backward_tile(
        jnp.where(is_late, q[0], r),
        jnp.where(is_late, r, k[0]),
        jnp.where(is_late, r2[0], v[0]),
        jnp.where(is_late, g[0], rg[0]),
        jnp.where(is_late, stat[0, 0], rstat[0, 0, 0]),
        jnp.where(is_late, delta[0, 0], rdelta[0, 0, 0]),
        False,
    )
    a, b = a.astype(BF16), b.astype(BF16)
    place = pl.program_id(0) * PAIR
    span = pl.num_programs(0) * PAIR
    send[0, :, pl.ds(pl.multiple_of(place, PAIR), PAIR)] = jnp.where(is_late, b, a)
    send[0, :, pl.ds(pl.multiple_of(span + place, PAIR), PAIR)] = c.astype(BF16)
    keep[0] = jnp.where(is_late, a, b)


def cols(length, b0=0, shift=0, low=lambda p: p):
    return pl.BlockSpec((1, length, PAIR), lambda p: (b0, 0, low(p) + shift))


def stats(length, shift=0, low=lambda p: p):
    return pl.BlockSpec((1, 1, 2, length), lambda p: (0, low(p) + shift, 0, 0))


SCALAR = pl.BlockSpec(memory_space=pltpu.SMEM)


def skip(kernel, count, *refs):
    kernel(*refs[count:])


def call(kernel, grid, ins, outs, shapes, cost, name, scratch=(), after=()):
    body = functools.partial(skip, kernel, len(after)) if after else kernel
    made = pl.pallas_call(
        body,
        grid=grid,
        in_specs=[pl.BlockSpec(memory_space=pl.ANY)] * len(after) + list(ins),
        out_specs=outs,
        out_shape=shapes,
        scratch_shapes=scratch,
        compiler_params=pltpu.CompilerParams(vmem_limit_bytes=VMEM),
        cost_estimate=pl.CostEstimate(
            flops=cost, bytes_accessed=cost // 256, transcendentals=cost // 256
        ),
        name=name,
    )
    return functools.partial(made, *after)


def gelu_parts(u):
    c = (2.0 / jnp.pi) ** 0.5
    u2 = u * u
    t = jnp.tanh(u * (c + (c * 0.044715) * u2))
    half = 0.5 + 0.5 * t
    value = u * half
    slope = half + 0.5 * u * (1.0 - t * t) * (c + (3 * c * 0.044715) * u2)
    return value, slope


ROWS = 256


def column_sum(v):
    return jnp.sum(v, axis=0, keepdims=True)


def middle_kernel(
    x, att, w_proj, b_proj, gain, shift, dz, w_up, b_up, w_down, b_down,
    out, dm, d_att, delta, sums, g_across, g_bias, g_down,
    middle, a2, a2_t, z, d_a2, h_all, du_all,
):
    step = pl.program_id(0)
    last = pl.num_programs(0) - 1
    parts = [slice(i, i + ROWS) for i in range(0, x.shape[0], ROWS)]

    @pl.when(step == 0)
    def _():
        for part in parts:
            m = x[part].astype(F32) + (dot(att[part], w_proj[...]) + b_proj[...])
            middle[part] = m
            normal, _ = norm_parts(m)
            a2[part] = (normal * gain[...] + shift[...]).astype(BF16)
        a2_t[...] = a2[...].T
        z[...] = jnp.zeros_like(z)
        d_a2[...] = jnp.zeros_like(d_a2)

    @pl.when(step < last)
    def _():
        for part in parts:
            u = dot(a2[part], w_up[...]) + b_up[...]
            value, slope = gelu_parts(u)
            h = value.astype(BF16)
            h_all[part] = h
            z[part] += dot(h, w_down[...])
            du = (dot(dz[part], w_down[...], NT) * slope).astype(BF16)
            du_all[part] = du
            d_a2[part] += dot(du, w_up[...], NT)
        du = du_all[...]
        g_bias[...] = column_sum(du.astype(F32))
        g_across[...] = dot(a2_t[...], du).astype(BF16)
        g_down[...] = dot(h_all[...].T, dz[...]).astype(BF16)

    @pl.when(step == last)
    def _():
        total = [jnp.zeros((1, x.shape[1]), F32)] * 4
        length = delta.shape[-1]
        for part in parts:
            m = middle[part]
            out[part] = (m + (z[part] + b_down[...])).astype(BF16)
            normal, inv = norm_parts(m)
            grad = d_a2[part]
            scaled = grad * gain[...]
            back = scaled - jnp.mean(scaled, axis=-1, keepdims=True)
            back = back - normal * jnp.mean(scaled * normal, axis=-1, keepdims=True)
            dz32 = dz[part].astype(F32)
            d = dz32 + back * inv
            dm[part] = d
            dy = d.astype(BF16)
            a2[part] = dy
            d_o = dot(dy, w_proj[...], NT).astype(BF16)
            d_att[part] = d_o
            prod = (d_o.astype(F32) * att[part].astype(F32)).T
            b, first = divmod(part.start, length)
            for p in range(delta.shape[1]):
                heads = [prod[i * HD : (i + 1) * HD] for i in (2 * p, 2 * p + 1)]
                delta[b, p, :, first : first + ROWS] = jnp.concatenate(
                    [column_sum(h) for h in heads], axis=0
                )
            new = [grad * normal, grad, dy.astype(F32), dz32]
            total = [t + column_sum(n) for t, n in zip(total, new)]
        sums[...] = jnp.concatenate(total + total, axis=0)
        g_across[...] = dot(att[...].T, a2[...]).astype(BF16)


def middle_part(x, att, up_proj, b_proj, gain, shift, dz, b_up, w_down, b_down, seqs):
    tokens, width = x.shape
    hidden = b_up.shape[0]
    part = width
    steps = hidden // part
    row = lambda v: v.reshape(1, -1)
    once = lambda shape, col=0: pl.BlockSpec(
        shape, lambda j: (0, col), pipeline_mode=pl.Buffered(1)
    )
    act, vec = once((tokens, width)), once((1, width))
    kept = lambda shape: pl.BlockSpec(shape, lambda j: (0,) * len(shape))
    at = lambda j: jnp.minimum(j, steps - 1)
    across = pl.BlockSpec((width, part), lambda j: (0, at(j)))
    down = pl.BlockSpec((part, width), lambda j: (at(j), 0))
    bias = pl.BlockSpec((1, part), lambda j: (0, at(j)))
    delta = (seqs, width // PAIR, 2, tokens // seqs)
    return call(
        middle_kernel,
        (steps + 1,),
        [act, act, once((width, width), steps), vec, vec, vec, act]
        + [across, bias, down, vec],
        [kept((tokens, width))] * 3
        + [kept(delta), kept((8, width))]
        + [pl.BlockSpec((width, part), lambda j: (0, j)), bias, down],
        [
            jax.ShapeDtypeStruct((tokens, width), BF16),
            jax.ShapeDtypeStruct((tokens, width), F32),
            jax.ShapeDtypeStruct((tokens, width), BF16),
            jax.ShapeDtypeStruct(delta, F32),
            jax.ShapeDtypeStruct((8, width), F32),
            jax.ShapeDtypeStruct((width, hidden + width), BF16),
            jax.ShapeDtypeStruct((1, hidden), F32),
            jax.ShapeDtypeStruct((hidden, width), BF16),
        ],
        12 * tokens * width * hidden,
        "middle_part",
        [
            pltpu.VMEM((tokens, width), F32),
            pltpu.VMEM((tokens, width), BF16),
            pltpu.VMEM((width, tokens), BF16),
            pltpu.VMEM((tokens, width), F32),
            pltpu.VMEM((tokens, width), F32),
            pltpu.VMEM((tokens, part), BF16),
            pltpu.VMEM((tokens, part), BF16),
        ],
    )(
        x, att, up_proj, row(b_proj), row(gain), row(shift), dz,
        up_proj, row(b_up), w_down, row(b_down),
    )


def join_kernel(first, late, a1, *refs):
    seqs = (len(refs) - 4) // 6
    near, far = refs[: 3 * seqs], refs[3 * seqs : 6 * seqs]
    dp, g, sums, a1_t = refs[6 * seqs :]
    c = pl.program_id(0) + first
    is_late = late[0] == 1
    is_early = late[0] == 0
    use_keep = (is_late & (c == 0)) | (is_early & (c == 3))
    use_got = (is_late & (c == 1)) | (is_early & ((c == 2) | (c == 4)))
    use_send = is_early & (c == 5)

    @pl.when(c == first)
    def _():
        a1_t[...] = a1[...].T

    length = near[0].shape[1]
    for b in range(seqs):
        q, k, v = [r[0] for r in near[3 * b : 3 * b + 3]]
        send, keep, got = [r[0] for r in far[3 * b : 3 * b + 3]]
        base = jnp.where(c < 2, q, jnp.where(c < 4, k, v)).astype(F32)
        add = jnp.where(use_keep, keep, jnp.where(use_got, got, send)).astype(F32)
        add = jnp.where(use_keep | use_got | use_send, add, 0.0)
        dp[b * length : (b + 1) * length] = (base + add).astype(BF16)
    whole = dp[...]
    sums[...] = column_sum(whole.astype(F32))
    g[...] = dot(a1_t[...], whole).astype(BF16)


def join(late_ref, a1, near, far, first, count, after):
    tokens, width = a1.shape
    seqs = len(near)
    length, half = near[0][0].shape[1], width // 2
    shape = (1, length, half)
    third = [
        pl.BlockSpec(shape, lambda c, t=t: (0, 0, jnp.clip(c + first - 2 * t, 0, 1))) for t in range(3)
    ]
    away = [
        pl.BlockSpec(shape, lambda c: (0, 0, 1)),
        pl.BlockSpec(shape, lambda c: (0, 0, 0)),
        pl.BlockSpec(shape, lambda c: (0, 0, jnp.where(c + first < 3, 0, 1))),
    ]
    return call(
        functools.partial(join_kernel, first),
        (count,),
        [SCALAR, pl.BlockSpec((tokens, width), lambda c: (0, 0))] + third * seqs + away * seqs,
        [
            pl.BlockSpec((tokens, half), lambda c: (0, c)),
            pl.BlockSpec((width, half), lambda c: (0, c)),
            pl.BlockSpec((1, half), lambda c: (0, c)),
        ],
        [
            jax.ShapeDtypeStruct((tokens, count * half), BF16),
            jax.ShapeDtypeStruct((width, count * half), BF16),
            jax.ShapeDtypeStruct((1, count * half), F32),
        ],
        2 * tokens * width * count * half,
        f"join_{first}",
        [pltpu.VMEM((width, tokens), BF16)],
        after,
    )(late_ref, a1, *[r for n in near for r in n], *[r for f in far for r in f])


def input_kernel(x, dm, front, back, w, gain, out, sums):
    @pl.when(pl.program_id(0) == 0)
    def _():
        sums[...] = jnp.zeros_like(sums)

    cut = front.shape[1]
    grad = dot(front[...], w[:, :cut], NT) + dot(back[...], w[:, cut:], NT)
    normal, inv = norm_parts(x[...].astype(F32))
    scaled = grad * gain[...]
    part = scaled - jnp.mean(scaled, axis=-1, keepdims=True)
    part = part - normal * jnp.mean(scaled * normal, axis=-1, keepdims=True)
    out[...] = dm[...] + part * inv
    sums[0:1] += column_sum(grad * normal)
    sums[1:2] += column_sum(grad)


def input_part(x, dm, front, back, w, gain, after):
    tokens, width = x.shape
    block = lambda v: pl.BlockSpec((ROWS, v.shape[1]), lambda i: (i, 0))
    kept = lambda shape: pl.BlockSpec(shape, lambda i: (0, 0))
    return call(
        input_kernel,
        (tokens // ROWS,),
        [block(x), block(dm), block(front), block(back)]
        + [pl.BlockSpec(w.shape, lambda i: (0, 0), pipeline_mode=pl.Buffered(1))]
        + [kept((1, width))],
        [block(x), kept((8, width))],
        [jax.ShapeDtypeStruct((tokens, width), F32), jax.ShapeDtypeStruct((8, width), F32)],
        2 * tokens * width * w.shape[1],
        "input_part",
        after=after,
    )(x, dm, front, back, w, gain.reshape(1, width))


def nothing(*refs):
    pass


def tie(value, *others):
    anywhere = pl.BlockSpec(memory_space=pl.ANY)
    return pl.pallas_call(
        nothing,
        in_specs=[anywhere] * (1 + len(others)),
        out_specs=anywhere,
        out_shape=jax.ShapeDtypeStruct(value.shape, value.dtype),
        input_output_aliases={0: 0},
        name="tie",
    )(value, *others)


class Cube:
    def __init__(self):
        self.seq = lax.axis_size("seq")
        self.fsdp = lax.axis_size("fsdp")
        self.count = self.seq * self.fsdp
        self.bits = self.fsdp.bit_length() - 1
        place = lax.axis_index("fsdp")
        seq = lax.axis_index("seq")
        self.me = (seq * self.fsdp + place).astype(jnp.int32).reshape(1)
        self.mine = [seq] + [(place >> (self.bits - 1 - i)) & 1 for i in range(self.bits)]
        self.far = list(range(1, self.bits - 1))
        self.y = self.bits - 1
        self.core = self.bits
        self.x = 0

    def mask(self, dim):
        return self.fsdp if dim == 0 else 1 << (self.bits - dim)

    def swap(self, value, dim):
        if dim == 0:
            return lax.ppermute(value, "seq", [(i, i ^ 1) for i in range(self.seq)])
        flip = self.mask(dim)
        return lax.ppermute(value, "fsdp", [(i, i ^ flip) for i in range(self.fsdp)])


class Gather:
    def __init__(self, cube, block, order):
        self.cube, self.order, self.at = cube, order, 0
        self.value = block[None]

    def step(self, *after):
        other = self.cube.swap(self.value, self.order[self.at])
        if after:
            other = tie(other, *after)
        self.at += 1
        self.value = jnp.concatenate([self.value, other], axis=0)
        return self.value

    def last(self, *after):
        self.other = self.cube.swap(self.value, self.order[self.at])
        if after:
            self.other = tie(self.other, *after)
        return self


def place_kernel(masks, flips, cuts, me, *refs):
    count = len(masks)
    ins, outs = refs[: 2 * count], refs[2 * count :]

    def body(i, carry):
        for source, low, high, target, first in cuts:
            place = me[0]
            for k, mask in enumerate(masks[source]):
                place = place ^ (((i >> k) & 1) * mask)
            for other in range(2):
                outs[target][place ^ (other * flips[source]), :, first : first + high - low] = ins[
                    2 * source + other
                ][i, :, low:high]
        return carry

    lax.fori_loop(0, ins[0].shape[0], body, 0)


def assemble(cube, gathers, cuts, widths, name):
    masks = [[cube.mask(d) for d in g.order[:-1]] for g in gathers]
    flips = [cube.mask(g.order[-1]) for g in gathers]
    rows = gathers[0].value.shape[1]
    args = [item for g in gathers for item in (g.value, g.other)]
    out = pl.pallas_call(
        functools.partial(place_kernel, masks, flips, cuts),
        in_specs=[SCALAR] + [pl.BlockSpec(memory_space=pltpu.VMEM)] * len(args),
        out_specs=[pl.BlockSpec(memory_space=pltpu.VMEM)] * len(widths),
        out_shape=[jax.ShapeDtypeStruct((cube.count, rows, w), BF16) for w in widths],
        compiler_params=pltpu.CompilerParams(vmem_limit_bytes=VMEM),
        cost_estimate=pl.CostEstimate(
            flops=0, bytes_accessed=4 * cube.count * rows * sum(widths), transcendentals=0
        ),
        name=name,
    )(cube.me, *args)
    return [o.reshape(cube.count * rows, -1) for o in out]


class Scatter:
    def __init__(self, cube, whole, order, wire=BF16):
        self.cube, self.order, self.at, self.wire = cube, order, 0, wire
        self.rows, self.tail = whole.shape[0] // cube.count, whole.shape[1:]
        self.value = whole.reshape((2,) * (cube.bits + 1) + (self.rows,) + self.tail)
        self.send()

    def send(self):
        dim = self.order[self.at]
        own = self.cube.mine[dim]
        sent = lax.dynamic_index_in_dim(self.value, 1 - own, dim, keepdims=True)
        self.sent = sent.astype(self.wire)
        self.got = self.cube.swap(self.sent, dim)

    def join(self, other):
        self.tail = self.tail[:-1] + (self.tail[-1] + other.tail[-1],)
        self.value = jnp.concatenate([self.value, other.value], axis=-1)
        self.send()

    def step(self, *after, send=True):
        if self.at == len(self.order):
            return self.value
        dim = self.order[self.at]
        got = tie(self.got, *after) if after else self.got
        keep = lax.dynamic_index_in_dim(self.value, self.cube.mine[dim], dim, keepdims=True)
        self.at += 1
        self.value = keep.astype(F32) + got.astype(F32)
        if self.at <= 2:
            self.value = self.value.astype(self.wire)
        if self.at < len(self.order) and send:
            self.send()
        else:
            self.sent = self.value
        return self.sent

    def result(self):
        while self.at < len(self.order):
            self.step()
        return self.value.reshape((self.rows,) + self.tail)


def norm_parts(values):
    centre = values - jnp.mean(values, axis=-1, keepdims=True)
    spread_ = jnp.mean(centre * centre, axis=-1, keepdims=True)
    inv = lax.rsqrt(spread_ + EPSILON)
    return centre * inv, inv


def per_device(
    inputs,
    out_grad,
    first_gain,
    first_shift,
    w_qkv,
    b_query,
    b_value,
    w_proj,
    b_proj,
    second_gain,
    second_shift,
    w_up,
    b_up,
    w_down,
    b_down,
):
    cube = Cube()
    late = lax.axis_index("seq")
    late_ref = late.astype(jnp.int32).reshape(1)
    seqs, length, width = inputs.shape
    tokens = seqs * length
    rows = w_qkv.shape[0]
    half = width // 2
    pairs = width // PAIR

    small = [first_gain, first_shift, b_query, b_value, b_proj, second_gain, second_shift, b_down]
    flat = jnp.concatenate(small + [b_up])
    packed_small = jnp.pad(flat, (0, 128 * rows - flat.shape[0])).reshape(rows, 128)
    cut = 3 * half
    x_last = cube.far + [cube.y, cube.x, cube.core]
    y_last = cube.far + [cube.x, cube.y, cube.core]
    front = Gather(cube, w_qkv[:, :cut], x_last)
    back = Gather(cube, jnp.concatenate([w_qkv[:, cut:], packed_small], axis=1), y_last)
    hidden = w_up.shape[1]
    up_proj = lax.all_gather(
        jnp.concatenate([w_up, w_proj], axis=1), ("seq", "fsdp"), axis=0, tiled=True
    )
    down_full = lax.all_gather(w_down, ("seq", "fsdp"), axis=0, tiled=True)
    for _ in x_last[:-1]:
        front.step(), back.step()
    front.last(), back.last()
    qkv_full, table = assemble(
        cube,
        [front, back],
        [
            (0, 0, cut, 0, 0),
            (1, 0, 3 * width - cut, 0, cut),
            (1, 3 * width - cut, 3 * width - cut + 128, 1, 0),
        ],
        [3 * width, 128],
        "place_qkv",
    )
    lines = -(-flat.shape[0] // 128)
    table = table.reshape(cube.count, rows, 128)[:, :lines].astype(F32)
    table = table.reshape(cube.count, lines * 128)
    vectors = table[:, : 8 * rows].reshape(cube.count, 8, rows)
    vectors = vectors.transpose(1, 0, 2).reshape(8, width)
    (gain_one, shift_one, query_bias, value_bias, proj_bias, gain_two, shift_two, down_bias) = [
        vectors[i] for i in range(8)
    ]
    up_bias = table[:, 8 * rows : flat.shape[0]].reshape(-1)

    x = inputs.astype(F32).reshape(tokens, width)
    normal_one, inv_one = norm_parts(x)
    a1 = (normal_one * gain_one + shift_one).astype(BF16)
    bias = jnp.concatenate([query_bias, jnp.zeros((width,), F32), value_bias])
    packed = (dot(a1, qkv_full) + bias).astype(BF16).reshape(seqs, length, 3 * width)

    forth = [(0, 1)]
    back_way = [(1, 0)]
    both_ways = [(0, 1), (1, 0)]
    early = late == 0
    hp = pairs // 2
    tile = 2 * 2 * length * length * PAIR
    whole_shape = jax.ShapeDtypeStruct((1, length, width), BF16)
    half_shape = jax.ShapeDtypeStruct((1, length, half), BF16)
    stat_shape = jax.ShapeDtypeStruct((1, pairs, 2, length), F32)
    half_stat = jax.ShapeDtypeStruct((1, hp, 2, length), F32)
    one, st = cols(length), stats(length)

    def own(b, third, high=0):
        return cols(length, b, third * pairs + high * hp)

    def local_forward(b, data):
        return call(
            local_forward_kernel,
            (pairs,),
            [own(b, 0), own(b, 1), own(b, 2)],
            [one, st],
            [whole_shape, stat_shape],
            tile * pairs,
            f"local_forward_{b}",
        )(data, data, data)

    def cross_forward(b, r, after):
        return call(
            cross_forward_kernel,
            (hp,),
            [SCALAR, own(b, 0), own(b, 1, 1), own(b, 2, 1), one, cols(length, 0, hp)],
            [one, st],
            [half_shape, half_stat],
            tile * hp,
            f"cross_forward_{b}",
            after=after,
        )(late_ref, packed, packed, packed, r, r)

    arrived, local, cross = [], [], []
    for b in range(seqs):
        row = packed[b : b + 1]
        send = jnp.concatenate(
            [
                jnp.where(early, row[:, :, width : width + half], row[:, :, half:width]),
                row[:, :, 2 * width : 2 * width + half],
            ],
            axis=2,
        )
        arrived.append(lax.ppermute(send, "seq", both_ways))
    for b in range(seqs):
        local.append(local_forward(b, packed))
    after = (local[-1][0],)
    for b in range(seqs):
        o2, l2 = cross_forward(b, arrived[b], after)
        after = (o2,)
        o3, l3 = lax.ppermute(o2, "seq", forth), lax.ppermute(l2, "seq", forth)
        cross.append((o2, l2, o3, l3))
    flat = [item for b in range(seqs) for item in local[b] + cross[b]]
    attended, stat_all = pl.pallas_call(
        merge_kernel,
        in_specs=[SCALAR] + [pl.BlockSpec(memory_space=pltpu.VMEM)] * len(flat),
        out_specs=[pl.BlockSpec(memory_space=pltpu.VMEM)] * 2,
        out_shape=[
            jax.ShapeDtypeStruct((seqs, length, width), BF16),
            jax.ShapeDtypeStruct((seqs, pairs, 2, length), F32),
        ],
        compiler_params=pltpu.CompilerParams(vmem_limit_bytes=VMEM),
        name="merge",
    )(late_ref, *flat)
    o_flat = attended.reshape(tokens, width)
    dz = out_grad.reshape(tokens, width)
    outputs, dm, d_att, delta_all, sums_two, whole_across, sum_up, whole_down = middle_part(
        inputs.reshape(tokens, width),
        o_flat,
        up_proj,
        proj_bias,
        gain_two,
        shift_two,
        dz,
        up_bias,
        down_full,
        down_bias,
        seqs,
    )
    y_first, x_first = y_last[::-1], x_last[::-1]
    mixed = [cube.core] + cube.far[-1:] + [cube.y] + cube.far[:-1][::-1] + [cube.x]
    grad_down = Scatter(cube, whole_down, mixed)
    grad_across = Scatter(cube, whole_across, y_first)
    d_att = d_att.reshape(seqs, length, width)
    rg = [lax.ppermute(d_att[b : b + 1, :, half:], "seq", back_way) for b in range(seqs)]
    sent = jnp.stack([stat_all[:, hp:], delta_all[:, hp:]])
    sent = lax.ppermute(sent, "seq", back_way)
    st_of = lambda b: pl.BlockSpec((1, 1, 2, length), lambda p: (b, p, 0, 0))
    far_of = lambda i, b: pl.BlockSpec((1, 1, 1, 2, length), lambda p: (i, b, p, 0, 0))
    def local_backward(b, after):
        return call(
            local_backward_kernel,
            (pairs,),
            [own(b, 0), own(b, 1), own(b, 2), cols(length, b), st_of(b), st_of(b)],
            [one, one, one],
            [whole_shape] * 3,
            3 * tile * pairs,
            f"local_backward_{b}",
            after=after,
        )(packed, packed, packed, d_att, stat_all, delta_all)

    def cross_backward(b, r, g, after):
        return call(
            cross_backward_kernel,
            (hp,),
            [SCALAR, own(b, 0), own(b, 1, 1), own(b, 2, 1), one, cols(length, 0, hp)]
            + [cols(length, b), one, st_of(b), st_of(b), far_of(0, b), far_of(1, b)],
            [pl.BlockSpec((1, length, width), lambda p: (0, 0, 0)), one],
            [whole_shape, half_shape],
            3 * tile * hp,
            f"cross_backward_{b}",
            after=after,
        )(late_ref, packed, packed, packed, r, r, d_att, g, stat_all, delta_all, sent, sent)

    near_grads, far_grads = [], []
    after = (grad_down.sent, grad_across.sent)
    for b in range(seqs):
        near_grads.append(local_backward(b, after))
        moved = ()
        if b == 0:
            moved = grad_down.step(), grad_across.step()
        send, keep = cross_backward(b, arrived[b], rg[b], (near_grads[b][0],))
        far_grads.append((send, keep, lax.ppermute(send, "seq", both_ways)))
        after = (send,) + moved
    grad_down.step(), grad_across.step()
    dp_front, g_front, sums_front = join(late_ref, a1, near_grads, far_grads, 0, 3, ())
    grad_front = Scatter(cube, g_front, x_first)
    moved = grad_front.step()
    dp_back, g_back, sums_back = join(late_ref, a1, near_grads, far_grads, 3, 3, (moved,))
    grad_back = Scatter(cube, g_back, y_first)
    moved = grad_down.step(grad_back.sent), grad_across.step(grad_back.sent)
    moved = (grad_back.step(*moved),) + moved
    input_grad, sums_one = input_part(
        inputs.reshape(tokens, width), dm, dp_front, dp_back, qkv_full, gain_one, moved
    )
    moved = grad_front.step(sums_one), grad_back.step(sums_one)
    moved = grad_down.step(*moved), grad_across.step(*moved)
    grad_front.step(*moved, send=False), grad_back.step(*moved, send=False)
    grad_front.join(grad_back)
    sums = jnp.concatenate([sums_front[0], sums_back[0]])
    grads_small = [
        sums_one[0],
        sums_one[1],
        sums[:width],
        sums[2 * width :],
        sums_two[2],
        sums_two[0],
        sums_two[1],
        sums_two[3],
    ]
    devices = width // rows
    pack = jnp.concatenate(
        [item.reshape(devices, rows) for item in grads_small]
        + [sum_up.reshape(devices, -1)],
        axis=1,
    )
    pack = lax.all_to_all(pack, ("seq", "fsdp"), split_axis=0, concat_axis=0, tiled=True)
    pack = jnp.sum(pack, axis=0)
    parts = [pack[i * rows : (i + 1) * rows] for i in range(8)]
    g_up_bias = pack[8 * rows :]
    across = grad_across.result()
    return (
        outputs.reshape(seqs, length, width),
        input_grad.reshape(seqs, length, width),
        parts[0],
        parts[1],
        grad_front.result(),
        parts[2],
        parts[3],
        across[:, hidden:],
        parts[4],
        parts[5],
        parts[6],
        across[:, :hidden],
        g_up_bias,
        grad_down.result(),
        parts[7],
    )


def solution(mesh):
    vector, matrix = P(("seq", "fsdp")), P(("seq", "fsdp"), None)
    tokens = P("fsdp", "seq", None)
    placed = (
        tokens,
        tokens,
        vector,
        vector,
        matrix,
        vector,
        vector,
        matrix,
        vector,
        vector,
        vector,
        matrix,
        vector,
        matrix,
        vector,
    )
    return jax.shard_map(
        per_device, mesh=mesh, in_specs=placed, out_specs=placed, check_vma=False
    )
```

```python
import functools

import jax
import jax.numpy as jnp
from jax import lax
from jax.experimental import pallas as pl
from jax.experimental.pallas import tpu as pltpu
from jax.sharding import PartitionSpec as P

H = 12
HD = 64
PAIR = 2 * HD
EPSILON = 1e-05
F32 = jnp.float32
BF16 = jnp.bfloat16
NT = (((1,), (1,)), ((), ()))
NN = (((1,), (0,)), ((), ()))
SUB = 256
VMEM = 56 * 1024 * 1024


def dot(a, b, dims=NN):
    return lax.dot_general(a, b, dims, preferred_element_type=F32)


def head_lanes(x, head):
    lane = lax.broadcasted_iota(jnp.int32, x.shape, 1)
    return jnp.where((lane // HD) == head, x, jnp.zeros_like(x))


def masked(scores, start):
    key = lax.broadcasted_iota(jnp.int32, scores.shape, 0)
    query = lax.broadcasted_iota(jnp.int32, scores.shape, 1) + start
    return jnp.where(key <= query, scores, -1e30)


def forward_tile(q, k, v, causal):
    q = q * jnp.asarray(HD**-0.5, q.dtype)
    v_t = v.T
    rows, keys = q.shape[0], k.shape[0]
    outs, stats = [], []
    for head in range(2):
        q_h = head_lanes(q, head)
        v_h = v_t[head * HD : (head + 1) * HD]
        out_h, stat_h = [], []
        for start in range(0, rows, SUB):
            used = start + SUB if causal else keys
            s = dot(k[:used], q_h[start : start + SUB], NT)
            if causal:
                s = masked(s, start)
            top = jnp.max(s, axis=0, keepdims=True)
            e = jnp.exp(s - top)
            total = jnp.sum(e, axis=0, keepdims=True)
            out_h.append(dot(v_h[:, :used], e.astype(BF16)) / total)
            stat_h.append(top + jnp.log(total))
        outs.append(jnp.concatenate(out_h, axis=1))
        stats.append(jnp.concatenate(stat_h, axis=1))
    return jnp.concatenate(outs, axis=0).T, jnp.concatenate(stats, axis=0)


def backward_tile(q, k, v, g, stat, delta, causal):
    q = q * jnp.asarray(HD**-0.5, q.dtype)
    k_t = k.T
    rows, keys = q.shape[0], k.shape[0]
    dq_heads = []
    pieces = [None] * (keys // SUB), [None] * (keys // SUB)

    def add(which, start, value):
        for i in range(value.shape[0] // SUB):
            part = value[i * SUB : (i + 1) * SUB]
            old = pieces[which][start + i]
            pieces[which][start + i] = part if old is None else old + part

    for head in range(2):
        q_h = head_lanes(q, head)
        g_h = head_lanes(g, head)
        k_h = k_t[head * HD : (head + 1) * HD]
        dq_h = []
        for start in range(0, rows, SUB):
            used = start + SUB if causal else keys
            cols = slice(start, start + SUB)
            s = dot(k[:used], q_h[cols], NT)
            if causal:
                s = masked(s, start)
            p = jnp.exp(s - stat[head : head + 1, cols])
            dp = dot(v[:used], g_h[cols], NT)
            ds = (p * (dp - delta[head : head + 1, cols])).astype(BF16)
            add(1, 0, dot(p.astype(BF16), g_h[cols]))
            add(0, 0, dot(ds, q_h[cols]))
            dq_h.append(dot(k_h[:, :used], ds))
        dq_heads.append(jnp.concatenate(dq_h, axis=1))
    dq = jnp.concatenate(dq_heads, axis=0).T * HD**-0.5
    return dq, jnp.concatenate(pieces[0], axis=0), jnp.concatenate(pieces[1], axis=0)


def local_forward_kernel(q, k, v, o, stat):
    out, lse = forward_tile(q[0], k[0], v[0], True)
    o[0] = out.astype(BF16)
    stat[0, 0] = lse


def cross_forward_kernel(late, q, k, v, r1, r2, o, stat):
    is_late = late[0] == 1
    r = r1[0]
    out, lse = forward_tile(
        jnp.where(is_late, q[0], r),
        jnp.where(is_late, r, k[0]),
        jnp.where(is_late, r2[0], v[0]),
        False,
    )
    o[0] = out.astype(BF16)
    stat[0, 0] = lse


def spread(rows, size):
    a = jnp.broadcast_to(rows[0:1], (HD, size))
    b = jnp.broadcast_to(rows[1:2], (HD, size))
    return jnp.concatenate([a, b], axis=0).T


def merge_kernel(late, *refs):
    o, stat = refs[-2:]
    seqs, pairs = stat.shape[:2]
    is_late = late[0] == 1
    for b in range(seqs):
        o1, l1, o2, l2, o3, l3 = refs[6 * b : 6 * b + 6]
        for p in range(pairs):
            near = p < pairs // 2
            at = p if near else p - pairs // 2
            here = slice(p * PAIR, (p + 1) * PAIR)
            there = slice(at * PAIR, (at + 1) * PAIR)
            first = l1[0, p]
            second = (l2 if near else l3)[0, at]
            gap = second - first
            weight = jnp.where(is_late, 1.0 / (1.0 + jnp.exp(-gap)), 0.0)
            both = jnp.maximum(first, second) + jnp.log(1.0 + jnp.exp(-jnp.abs(gap)))
            stat[b, p] = jnp.where(is_late, both, first)
            own = o1[0, :, here].astype(F32)
            other = (o2 if near else o3)[0, :, there].astype(F32)
            o[b, :, here] = (own + spread(weight, own.shape[0]) * (other - own)).astype(BF16)


def local_backward_kernel(q, k, v, g, stat, delta, dq, dk, dv):
    a, b, c = backward_tile(q[0], k[0], v[0], g[0], stat[0, 0], delta[0, 0], True)
    dq[0] = a.astype(BF16)
    dk[0] = b.astype(BF16)
    dv[0] = c.astype(BF16)


def cross_backward_kernel(
    late, q, k, v, r1, r2, g, rg, stat, delta, rstat, rdelta, send, keep
):
    is_late = late[0] == 1
    r = r1[0]
    a, b, c = backward_tile(
        jnp.where(is_late, q[0], r),
        jnp.where(is_late, r, k[0]),
        jnp.where(is_late, r2[0], v[0]),
        jnp.where(is_late, g[0], rg[0]),
        jnp.where(is_late, stat[0, 0], rstat[0, 0, 0]),
        jnp.where(is_late, delta[0, 0], rdelta[0, 0, 0]),
        False,
    )
    a, b = a.astype(BF16), b.astype(BF16)
    place = pl.program_id(0) * PAIR
    span = pl.num_programs(0) * PAIR
    send[0, :, pl.ds(pl.multiple_of(place, PAIR), PAIR)] = jnp.where(is_late, b, a)
    send[0, :, pl.ds(pl.multiple_of(span + place, PAIR), PAIR)] = c.astype(BF16)
    keep[0] = jnp.where(is_late, a, b)


def cols(length, b0=0, shift=0, low=lambda p: p):
    return pl.BlockSpec((1, length, PAIR), lambda p: (b0, 0, low(p) + shift))


def stats(length, shift=0, low=lambda p: p):
    return pl.BlockSpec((1, 1, 2, length), lambda p: (0, low(p) + shift, 0, 0))


SCALAR = pl.BlockSpec(memory_space=pltpu.SMEM)


def skip(kernel, count, *refs):
    kernel(*refs[count:])


def call(kernel, grid, ins, outs, shapes, cost, name, scratch=(), after=()):
    body = functools.partial(skip, kernel, len(after)) if after else kernel
    made = pl.pallas_call(
        body,
        grid=grid,
        in_specs=[pl.BlockSpec(memory_space=pl.ANY)] * len(after) + list(ins),
        out_specs=outs,
        out_shape=shapes,
        scratch_shapes=scratch,
        compiler_params=pltpu.CompilerParams(vmem_limit_bytes=VMEM),
        cost_estimate=pl.CostEstimate(
            flops=cost, bytes_accessed=cost // 256, transcendentals=cost // 256
        ),
        name=name,
    )
    return functools.partial(made, *after)


def gelu_parts(u):
    c = (2.0 / jnp.pi) ** 0.5
    u2 = u * u
    t = jnp.tanh(u * (c + (c * 0.044715) * u2))
    half = 0.5 + 0.5 * t
    value = u * half
    slope = half + 0.5 * u * (1.0 - t * t) * (c + (3 * c * 0.044715) * u2)
    return value, slope


ROWS = 256


def column_sum(v):
    return jnp.sum(v, axis=0, keepdims=True)


def middle_kernel(
    x, att, w_proj, b_proj, gain, shift, dz, w_up, b_up, w_down, b_down,
    out, dm, d_att, delta, sums, g_across, g_bias, g_down,
    middle, a2, a2_t, z, d_a2, h_all, du_all,
):
    step = pl.program_id(0)
    last = pl.num_programs(0) - 1
    parts = [slice(i, i + ROWS) for i in range(0, x.shape[0], ROWS)]

    @pl.when(step == 0)
    def _():
        for part in parts:
            m = x[part].astype(F32) + (dot(att[part], w_proj[...]) + b_proj[...])
            middle[part] = m
            normal, _ = norm_parts(m)
            a2[part] = (normal * gain[...] + shift[...]).astype(BF16)
        a2_t[...] = a2[...].T
        z[...] = jnp.zeros_like(z)
        d_a2[...] = jnp.zeros_like(d_a2)

    @pl.when(step < last)
    def _():
        for part in parts:
            u = dot(a2[part], w_up[...]) + b_up[...]
            value, slope = gelu_parts(u)
            h = value.astype(BF16)
            h_all[part] = h
            z[part] += dot(h, w_down[...])
            du = (dot(dz[part], w_down[...], NT) * slope).astype(BF16)
            du_all[part] = du
            d_a2[part] += dot(du, w_up[...], NT)
        du = du_all[...]
        g_bias[...] = column_sum(du.astype(F32))
        g_across[...] = dot(a2_t[...], du).astype(BF16)
        g_down[...] = dot(h_all[...].T, dz[...]).astype(BF16)

    @pl.when(step == last)
    def _():
        total = [jnp.zeros((1, x.shape[1]), F32)] * 4
        length = delta.shape[-1]
        for part in parts:
            m = middle[part]
            out[part] = (m + (z[part] + b_down[...])).astype(BF16)
            normal, inv = norm_parts(m)
            grad = d_a2[part]
            scaled = grad * gain[...]
            back = scaled - jnp.mean(scaled, axis=-1, keepdims=True)
            back = back - normal * jnp.mean(scaled * normal, axis=-1, keepdims=True)
            dz32 = dz[part].astype(F32)
            d = dz32 + back * inv
            dm[part] = d
            dy = d.astype(BF16)
            a2[part] = dy
            d_o = dot(dy, w_proj[...], NT).astype(BF16)
            d_att[part] = d_o
            prod = (d_o.astype(F32) * att[part].astype(F32)).T
            b, first = divmod(part.start, length)
            for p in range(delta.shape[1]):
                heads = [prod[i * HD : (i + 1) * HD] for i in (2 * p, 2 * p + 1)]
                delta[b, p, :, first : first + ROWS] = jnp.concatenate(
                    [column_sum(h) for h in heads], axis=0
                )
            new = [grad * normal, grad, dy.astype(F32), dz32]
            total = [t + column_sum(n) for t, n in zip(total, new)]
        sums[...] = jnp.concatenate(total + total, axis=0)
        g_across[...] = dot(att[...].T, a2[...]).astype(BF16)


def middle_part(x, att, up_proj, b_proj, gain, shift, dz, b_up, w_down, b_down, seqs):
    tokens, width = x.shape
    hidden = b_up.shape[0]
    part = width
    steps = hidden // part
    row = lambda v: v.reshape(1, -1)
    once = lambda shape, col=0: pl.BlockSpec(
        shape, lambda j: (0, col), pipeline_mode=pl.Buffered(1)
    )
    act, vec = once((tokens, width)), once((1, width))
    kept = lambda shape: pl.BlockSpec(shape, lambda j: (0,) * len(shape))
    at = lambda j: jnp.minimum(j, steps - 1)
    across = pl.BlockSpec((width, part), lambda j: (0, at(j)))
    down = pl.BlockSpec((part, width), lambda j: (at(j), 0))
    bias = pl.BlockSpec((1, part), lambda j: (0, at(j)))
    delta = (seqs, width // PAIR, 2, tokens // seqs)
    return call(
        middle_kernel,
        (steps + 1,),
        [act, act, once((width, width), steps), vec, vec, vec, act]
        + [across, bias, down, vec],
        [kept((tokens, width))] * 3
        + [kept(delta), kept((8, width))]
        + [pl.BlockSpec((width, part), lambda j: (0, j)), bias, down],
        [
            jax.ShapeDtypeStruct((tokens, width), BF16),
            jax.ShapeDtypeStruct((tokens, width), F32),
            jax.ShapeDtypeStruct((tokens, width), BF16),
            jax.ShapeDtypeStruct(delta, F32),
            jax.ShapeDtypeStruct((8, width), F32),
            jax.ShapeDtypeStruct((width, hidden + width), BF16),
            jax.ShapeDtypeStruct((1, hidden), F32),
            jax.ShapeDtypeStruct((hidden, width), BF16),
        ],
        12 * tokens * width * hidden,
        "middle_part",
        [
            pltpu.VMEM((tokens, width), F32),
            pltpu.VMEM((tokens, width), BF16),
            pltpu.VMEM((width, tokens), BF16),
            pltpu.VMEM((tokens, width), F32),
            pltpu.VMEM((tokens, width), F32),
            pltpu.VMEM((tokens, part), BF16),
            pltpu.VMEM((tokens, part), BF16),
        ],
    )(
        x, att, up_proj, row(b_proj), row(gain), row(shift), dz,
        up_proj, row(b_up), w_down, row(b_down),
    )


def join_kernel(first, late, a1, *refs):
    seqs = (len(refs) - 4) // 6
    near, far = refs[: 3 * seqs], refs[3 * seqs : 6 * seqs]
    dp, g, sums, a1_t = refs[6 * seqs :]
    c = pl.program_id(0) + first
    is_late = late[0] == 1
    is_early = late[0] == 0
    use_keep = (is_late & (c == 0)) | (is_early & (c == 3))
    use_got = (is_late & (c == 1)) | (is_early & ((c == 2) | (c == 4)))
    use_send = is_early & (c == 5)

    @pl.when(c == first)
    def _():
        a1_t[...] = a1[...].T

    length = near[0].shape[1]
    for b in range(seqs):
        q, k, v = [r[0] for r in near[3 * b : 3 * b + 3]]
        send, keep, got = [r[0] for r in far[3 * b : 3 * b + 3]]
        base = jnp.where(c < 2, q, jnp.where(c < 4, k, v)).astype(F32)
        add = jnp.where(use_keep, keep, jnp.where(use_got, got, send)).astype(F32)
        add = jnp.where(use_keep | use_got | use_send, add, 0.0)
        dp[b * length : (b + 1) * length] = (base + add).astype(BF16)
    whole = dp[...]
    sums[...] = column_sum(whole.astype(F32))
    g[...] = dot(a1_t[...], whole).astype(BF16)


def join(late_ref, a1, near, far, first, count, after):
    tokens, width = a1.shape
    seqs = len(near)
    length, half = near[0][0].shape[1], width // 2
    shape = (1, length, half)
    third = [
        pl.BlockSpec(shape, lambda c, t=t: (0, 0, jnp.clip(c + first - 2 * t, 0, 1))) for t in range(3)
    ]
    away = [
        pl.BlockSpec(shape, lambda c: (0, 0, 1)),
        pl.BlockSpec(shape, lambda c: (0, 0, 0)),
        pl.BlockSpec(shape, lambda c: (0, 0, jnp.where(c + first < 3, 0, 1))),
    ]
    return call(
        functools.partial(join_kernel, first),
        (count,),
        [SCALAR, pl.BlockSpec((tokens, width), lambda c: (0, 0))] + third * seqs + away * seqs,
        [
            pl.BlockSpec((tokens, half), lambda c: (0, c)),
            pl.BlockSpec((width, half), lambda c: (0, c)),
            pl.BlockSpec((1, half), lambda c: (0, c)),
        ],
        [
            jax.ShapeDtypeStruct((tokens, count * half), BF16),
            jax.ShapeDtypeStruct((width, count * half), BF16),
            jax.ShapeDtypeStruct((1, count * half), F32),
        ],
        2 * tokens * width * count * half,
        f"join_{first}",
        [pltpu.VMEM((width, tokens), BF16)],
        after,
    )(late_ref, a1, *[r for n in near for r in n], *[r for f in far for r in f])


def input_kernel(x, dm, front, back, w, gain, out, sums):
    @pl.when(pl.program_id(0) == 0)
    def _():
        sums[...] = jnp.zeros_like(sums)

    cut = front.shape[1]
    grad = dot(front[...], w[:, :cut], NT) + dot(back[...], w[:, cut:], NT)
    normal, inv = norm_parts(x[...].astype(F32))
    scaled = grad * gain[...]
    part = scaled - jnp.mean(scaled, axis=-1, keepdims=True)
    part = part - normal * jnp.mean(scaled * normal, axis=-1, keepdims=True)
    out[...] = dm[...] + part * inv
    sums[0:1] += column_sum(grad * normal)
    sums[1:2] += column_sum(grad)


def input_part(x, dm, front, back, w, gain, after):
    tokens, width = x.shape
    block = lambda v: pl.BlockSpec((ROWS, v.shape[1]), lambda i: (i, 0))
    kept = lambda shape: pl.BlockSpec(shape, lambda i: (0, 0))
    return call(
        input_kernel,
        (tokens // ROWS,),
        [block(x), block(dm), block(front), block(back)]
        + [pl.BlockSpec(w.shape, lambda i: (0, 0), pipeline_mode=pl.Buffered(1))]
        + [kept((1, width))],
        [block(x), kept((8, width))],
        [jax.ShapeDtypeStruct((tokens, width), F32), jax.ShapeDtypeStruct((8, width), F32)],
        2 * tokens * width * w.shape[1],
        "input_part",
        after=after,
    )(x, dm, front, back, w, gain.reshape(1, width))


def nothing(*refs):
    pass


def tie(value, *others):
    anywhere = pl.BlockSpec(memory_space=pl.ANY)
    return pl.pallas_call(
        nothing,
        in_specs=[anywhere] * (1 + len(others)),
        out_specs=anywhere,
        out_shape=jax.ShapeDtypeStruct(value.shape, value.dtype),
        input_output_aliases={0: 0},
        name="tie",
    )(value, *others)


class Cube:
    def __init__(self):
        self.seq = lax.axis_size("seq")
        self.fsdp = lax.axis_size("fsdp")
        self.count = self.seq * self.fsdp
        self.bits = self.fsdp.bit_length() - 1
        place = lax.axis_index("fsdp")
        seq = lax.axis_index("seq")
        self.me = (seq * self.fsdp + place).astype(jnp.int32).reshape(1)
        self.mine = [seq] + [(place >> (self.bits - 1 - i)) & 1 for i in range(self.bits)]
        self.far = list(range(1, self.bits - 1))
        self.y = self.bits - 1
        self.core = self.bits
        self.x = 0

    def mask(self, dim):
        return self.fsdp if dim == 0 else 1 << (self.bits - dim)

    def swap(self, value, dim):
        if dim == 0:
            return lax.ppermute(value, "seq", [(i, i ^ 1) for i in range(self.seq)])
        flip = self.mask(dim)
        return lax.ppermute(value, "fsdp", [(i, i ^ flip) for i in range(self.fsdp)])


class Gather:
    def __init__(self, cube, block, order):
        self.cube, self.order, self.at = cube, order, 0
        self.value = block[None]

    def step(self, *after):
        other = self.cube.swap(self.value, self.order[self.at])
        if after:
            other = tie(other, *after)
        self.at += 1
        self.value = jnp.concatenate([self.value, other], axis=0)
        return self.value

    def last(self, *after):
        self.other = self.cube.swap(self.value, self.order[self.at])
        if after:
            self.other = tie(self.other, *after)
        return self


def place_kernel(masks, flips, cuts, me, *refs):
    count = len(masks)
    ins, outs = refs[: 2 * count], refs[2 * count :]

    def body(i, carry):
        for source, low, high, target, first in cuts:
            place = me[0]
            for k, mask in enumerate(masks[source]):
                place = place ^ (((i >> k) & 1) * mask)
            for other in range(2):
                outs[target][place ^ (other * flips[source]), :, first : first + high - low] = ins[
                    2 * source + other
                ][i, :, low:high]
        return carry

    lax.fori_loop(0, ins[0].shape[0], body, 0)


def assemble(cube, gathers, cuts, widths, name):
    masks = [[cube.mask(d) for d in g.order[:-1]] for g in gathers]
    flips = [cube.mask(g.order[-1]) for g in gathers]
    rows = gathers[0].value.shape[1]
    args = [item for g in gathers for item in (g.value, g.other)]
    out = pl.pallas_call(
        functools.partial(place_kernel, masks, flips, cuts),
        in_specs=[SCALAR] + [pl.BlockSpec(memory_space=pltpu.VMEM)] * len(args),
        out_specs=[pl.BlockSpec(memory_space=pltpu.VMEM)] * len(widths),
        out_shape=[jax.ShapeDtypeStruct((cube.count, rows, w), BF16) for w in widths],
        compiler_params=pltpu.CompilerParams(vmem_limit_bytes=VMEM),
        cost_estimate=pl.CostEstimate(
            flops=0, bytes_accessed=4 * cube.count * rows * sum(widths), transcendentals=0
        ),
        name=name,
    )(cube.me, *args)
    return [o.reshape(cube.count * rows, -1) for o in out]


class Scatter:
    def __init__(self, cube, whole, order, wire=BF16):
        self.cube, self.order, self.at, self.wire = cube, order, 0, wire
        self.rows, self.tail = whole.shape[0] // cube.count, whole.shape[1:]
        self.value = whole.reshape((2,) * (cube.bits + 1) + (self.rows,) + self.tail)
        self.send()

    def send(self):
        dim = self.order[self.at]
        own = self.cube.mine[dim]
        sent = lax.dynamic_index_in_dim(self.value, 1 - own, dim, keepdims=True)
        self.sent = sent.astype(self.wire)
        self.got = self.cube.swap(self.sent, dim)

    def join(self, other):
        self.tail = self.tail[:-1] + (self.tail[-1] + other.tail[-1],)
        self.value = jnp.concatenate([self.value, other.value], axis=-1)
        self.send()

    def step(self, *after, send=True):
        if self.at == len(self.order):
            return self.value
        dim = self.order[self.at]
        got = tie(self.got, *after) if after else self.got
        keep = lax.dynamic_index_in_dim(self.value, self.cube.mine[dim], dim, keepdims=True)
        self.at += 1
        self.value = keep.astype(F32) + got.astype(F32)
        if self.at <= 2:
            self.value = self.value.astype(self.wire)
        if self.at < len(self.order) and send:
            self.send()
        else:
            self.sent = self.value
        return self.sent

    def result(self):
        while self.at < len(self.order):
            self.step()
        return self.value.reshape((self.rows,) + self.tail)


def norm_parts(values):
    centre = values - jnp.mean(values, axis=-1, keepdims=True)
    spread_ = jnp.mean(centre * centre, axis=-1, keepdims=True)
    inv = lax.rsqrt(spread_ + EPSILON)
    return centre * inv, inv


def per_device(
    inputs,
    out_grad,
    first_gain,
    first_shift,
    w_qkv,
    b_query,
    b_value,
    w_proj,
    b_proj,
    second_gain,
    second_shift,
    w_up,
    b_up,
    w_down,
    b_down,
):
    cube = Cube()
    late = lax.axis_index("seq")
    late_ref = late.astype(jnp.int32).reshape(1)
    seqs, length, width = inputs.shape
    tokens = seqs * length
    rows = w_qkv.shape[0]
    half = width // 2
    pairs = width // PAIR

    small = [first_gain, first_shift, b_query, b_value, b_proj, second_gain, second_shift, b_down]
    flat = jnp.concatenate(small + [b_up])
    packed_small = jnp.pad(flat, (0, 128 * rows - flat.shape[0])).reshape(rows, 128)
    cut = 3 * half
    x_last = cube.far + [cube.y, cube.x, cube.core]
    y_last = cube.far + [cube.x, cube.y, cube.core]
    front = Gather(cube, w_qkv[:, :cut], x_last)
    back = Gather(cube, jnp.concatenate([w_qkv[:, cut:], packed_small], axis=1), y_last)
    hidden = w_up.shape[1]
    up_proj = lax.all_gather(
        jnp.concatenate([w_up, w_proj], axis=1), ("seq", "fsdp"), axis=0, tiled=True
    )
    down_full = lax.all_gather(w_down, ("seq", "fsdp"), axis=0, tiled=True)
    for _ in x_last[:-1]:
        front.step(), back.step()
    front.last(), back.last()
    qkv_full, table = assemble(
        cube,
        [front, back],
        [
            (0, 0, cut, 0, 0),
            (1, 0, 3 * width - cut, 0, cut),
            (1, 3 * width - cut, 3 * width - cut + 128, 1, 0),
        ],
        [3 * width, 128],
        "place_qkv",
    )
    lines = -(-flat.shape[0] // 128)
    table = table.reshape(cube.count, rows, 128)[:, :lines].astype(F32)
    table = table.reshape(cube.count, lines * 128)
    vectors = table[:, : 8 * rows].reshape(cube.count, 8, rows)
    vectors = vectors.transpose(1, 0, 2).reshape(8, width)
    (gain_one, shift_one, query_bias, value_bias, proj_bias, gain_two, shift_two, down_bias) = [
        vectors[i] for i in range(8)
    ]
    up_bias = table[:, 8 * rows : flat.shape[0]].reshape(-1)

    x = inputs.astype(F32).reshape(tokens, width)
    normal_one, inv_one = norm_parts(x)
    a1 = (normal_one * gain_one + shift_one).astype(BF16)
    bias = jnp.concatenate([query_bias, jnp.zeros((width,), F32), value_bias])
    packed = (dot(a1, qkv_full) + bias).astype(BF16).reshape(seqs, length, 3 * width)

    forth = [(0, 1)]
    back_way = [(1, 0)]
    both_ways = [(0, 1), (1, 0)]
    early = late == 0
    hp = pairs // 2
    tile = 2 * 2 * length * length * PAIR
    whole_shape = jax.ShapeDtypeStruct((1, length, width), BF16)
    half_shape = jax.ShapeDtypeStruct((1, length, half), BF16)
    stat_shape = jax.ShapeDtypeStruct((1, pairs, 2, length), F32)
    half_stat = jax.ShapeDtypeStruct((1, hp, 2, length), F32)
    one, st = cols(length), stats(length)

    def own(b, third, high=0):
        return cols(length, b, third * pairs + high * hp)

    def local_forward(b, data):
        return call(
            local_forward_kernel,
            (pairs,),
            [own(b, 0), own(b, 1), own(b, 2)],
            [one, st],
            [whole_shape, stat_shape],
            tile * pairs,
            f"local_forward_{b}",
        )(data, data, data)

    def cross_forward(b, r, after):
        return call(
            cross_forward_kernel,
            (hp,),
            [SCALAR, own(b, 0), own(b, 1, 1), own(b, 2, 1), one, cols(length, 0, hp)],
            [one, st],
            [half_shape, half_stat],
            tile * hp,
            f"cross_forward_{b}",
            after=after,
        )(late_ref, packed, packed, packed, r, r)

    arrived, local, cross = [], [], []
    for b in range(seqs):
        row = packed[b : b + 1]
        send = jnp.concatenate(
            [
                jnp.where(early, row[:, :, width : width + half], row[:, :, half:width]),
                row[:, :, 2 * width : 2 * width + half],
            ],
            axis=2,
        )
        arrived.append(lax.ppermute(send, "seq", both_ways))
    for b in range(seqs):
        local.append(local_forward(b, packed))
    after = tuple(o1 for o1, _ in local)
    for b in range(seqs):
        o2, l2 = cross_forward(b, arrived[b], after)
        o3, l3 = lax.ppermute(o2, "seq", forth), lax.ppermute(l2, "seq", forth)
        cross.append((o2, l2, o3, l3))
    flat = [item for b in range(seqs) for item in local[b] + cross[b]]
    attended, stat_all = pl.pallas_call(
        merge_kernel,
        in_specs=[SCALAR] + [pl.BlockSpec(memory_space=pltpu.VMEM)] * len(flat),
        out_specs=[pl.BlockSpec(memory_space=pltpu.VMEM)] * 2,
        out_shape=[
            jax.ShapeDtypeStruct((seqs, length, width), BF16),
            jax.ShapeDtypeStruct((seqs, pairs, 2, length), F32),
        ],
        compiler_params=pltpu.CompilerParams(vmem_limit_bytes=VMEM),
        name="merge",
    )(late_ref, *flat)
    o_flat = attended.reshape(tokens, width)
    dz = out_grad.reshape(tokens, width)
    outputs, dm, d_att, delta_all, sums_two, whole_across, sum_up, whole_down = middle_part(
        inputs.reshape(tokens, width),
        o_flat,
        up_proj,
        proj_bias,
        gain_two,
        shift_two,
        dz,
        up_bias,
        down_full,
        down_bias,
        seqs,
    )
    y_first, x_first = y_last[::-1], x_last[::-1]
    mixed = [cube.core] + cube.far[-1:] + [cube.y] + cube.far[:-1][::-1] + [cube.x]
    grad_down = Scatter(cube, whole_down, mixed)
    grad_across = Scatter(cube, whole_across, y_first)
    d_att = d_att.reshape(seqs, length, width)
    rg = [lax.ppermute(d_att[b : b + 1, :, half:], "seq", back_way) for b in range(seqs)]
    sent = jnp.stack([stat_all[:, hp:], delta_all[:, hp:]])
    sent = lax.ppermute(sent, "seq", back_way)
    st_of = lambda b: pl.BlockSpec((1, 1, 2, length), lambda p: (b, p, 0, 0))
    far_of = lambda i, b: pl.BlockSpec((1, 1, 1, 2, length), lambda p: (i, b, p, 0, 0))
    def local_backward(b, after):
        return call(
            local_backward_kernel,
            (pairs,),
            [own(b, 0), own(b, 1), own(b, 2), cols(length, b), st_of(b), st_of(b)],
            [one, one, one],
            [whole_shape] * 3,
            3 * tile * pairs,
            f"local_backward_{b}",
            after=after,
        )(packed, packed, packed, d_att, stat_all, delta_all)

    def cross_backward(b, r, g, after):
        return call(
            cross_backward_kernel,
            (hp,),
            [SCALAR, own(b, 0), own(b, 1, 1), own(b, 2, 1), one, cols(length, 0, hp)]
            + [cols(length, b), one, st_of(b), st_of(b), far_of(0, b), far_of(1, b)],
            [pl.BlockSpec((1, length, width), lambda p: (0, 0, 0)), one],
            [whole_shape, half_shape],
            3 * tile * hp,
            f"cross_backward_{b}",
            after=after,
        )(late_ref, packed, packed, packed, r, r, d_att, g, stat_all, delta_all, sent, sent)

    near_grads, far_grads = [], []
    after = (grad_down.sent, grad_across.sent)
    for b in range(seqs):
        near_grads.append(local_backward(b, after))
        moved = ()
        if b == 0:
            moved = grad_down.step(), grad_across.step()
        send, keep = cross_backward(b, arrived[b], rg[b], (near_grads[b][0],))
        far_grads.append((send, keep, lax.ppermute(send, "seq", both_ways)))
        after = (send,) + moved
    grad_down.step(), grad_across.step()
    dp_front, g_front, sums_front = join(late_ref, a1, near_grads, far_grads, 0, 3, ())
    grad_front = Scatter(cube, g_front, x_first)
    moved = grad_front.step()
    dp_back, g_back, sums_back = join(late_ref, a1, near_grads, far_grads, 3, 3, (moved,))
    grad_back = Scatter(cube, g_back, y_first)
    moved = grad_down.step(grad_back.sent), grad_across.step(grad_back.sent)
    moved = (grad_back.step(*moved),) + moved
    input_grad, sums_one = input_part(
        inputs.reshape(tokens, width), dm, dp_front, dp_back, qkv_full, gain_one, moved
    )
    moved = grad_front.step(sums_one), grad_back.step(sums_one)
    moved = grad_down.step(*moved), grad_across.step(*moved)
    grad_front.step(*moved, send=False), grad_back.step(*moved, send=False)
    grad_front.join(grad_back)
    sums = jnp.concatenate([sums_front[0], sums_back[0]])
    grads_small = [
        sums_one[0],
        sums_one[1],
        sums[:width],
        sums[2 * width :],
        sums_two[2],
        sums_two[0],
        sums_two[1],
        sums_two[3],
    ]
    devices = width // rows
    pack = jnp.concatenate(
        [item.reshape(devices, rows) for item in grads_small]
        + [sum_up.reshape(devices, -1)],
        axis=1,
    )
    pack = lax.all_to_all(pack, ("seq", "fsdp"), split_axis=0, concat_axis=0, tiled=True)
    pack = jnp.sum(pack, axis=0)
    parts = [pack[i * rows : (i + 1) * rows] for i in range(8)]
    g_up_bias = pack[8 * rows :]
    across = grad_across.result()
    return (
        outputs.reshape(seqs, length, width),
        input_grad.reshape(seqs, length, width),
        parts[0],
        parts[1],
        grad_front.result(),
        parts[2],
        parts[3],
        across[:, hidden:],
        parts[4],
        parts[5],
        parts[6],
        across[:, :hidden],
        g_up_bias,
        grad_down.result(),
        parts[7],
    )


def solution(mesh):
    vector, matrix = P(("seq", "fsdp")), P(("seq", "fsdp"), None)
    tokens = P("fsdp", "seq", None)
    placed = (
        tokens,
        tokens,
        vector,
        vector,
        matrix,
        vector,
        vector,
        matrix,
        vector,
        vector,
        vector,
        matrix,
        vector,
        matrix,
        vector,
    )
    return jax.shard_map(
        per_device, mesh=mesh, in_specs=placed, out_specs=placed, check_vma=False
    )
```
